256 devices in a mesh: seq: 16 (over z, core), chan: 16 (over y, x).
Axes of the slice: x: 4, y: 4, z: 8, core: 2. Of those that a mesh axis runs over, the one named last changes fastest.
Arguments:
- proj: bfloat16 [3, 8192, 8192], P(None, 'seq', 'chan'), may hold values from -6 to 6
- short_filters: float32 [3, 7, 8192], P(None, None, 'chan'), may hold values from -2.4 to 2.4
- long_filter: float32 [128, 8192], P(None, 'chan')
- out_weight: bfloat16 [8192, 8192], P('chan', 'seq'), may hold values from -0.0625 to 0.0625
- cotangent: bfloat16 [8192, 8192], P('seq', 'chan'), may hold values from -6 to 6
- pack: int32 [16], replicated, may hold values from 0 to 15, as said below
- since_start: int32 [8192], P('seq'), may hold values from 0 to 2047, as said below
- until_end: int32 [8192], P('seq'), may hold values from 0 to 2047, as said below
Outputs:
- mixed: bfloat16 [8192, 8192], P('seq', 'chan')
- grad_proj: bfloat16 [3, 8192, 8192], P(None, 'seq', 'chan')
The draws below stay inside these ranges and needn't reach their ends.
Inputs may be any that keep to these rules, and one draw needn't show every extreme that they name: `pack`: each logical piece of 512 tokens appears once. `since_start`: for each stored token, the number of tokens of its document before it in logical order; the first logical token has 0. `until_end`: for each stored token, the number of tokens of its document after it in logical order; the last logical token has 0. Consistent with since_start.
All inputs are finite; a program needn't handle non-finite values.
Results may differ from the reference program's by a relative error of at most 0.02.
Values may be sent and summed in bfloat16 or wider, within the bound.
A program may use at most 192 MiB of HBM per device.

```python
import math
import jax
import jax.numpy as jnp
from jax import lax

D = 8192
FILT = 128
SHORT = 7
TOK = 512
TOKENS = 8192
N_SEQ = 16


spacing = 3000


def layout_draw(key):
    first_key, second_key, third_key = jax.random.split(key, 3)
    pack = jax.random.permutation(first_key, N_SEQ).astype(jnp.int32)
    positions = jnp.arange(TOKENS, dtype=jnp.int32)
    quarter = TOKENS // 4
    first_pieces = N_SEQ // 4
    chosen = jax.random.randint(third_key, (2,), 0, 1 << 20)
    inner_piece = first_pieces + chosen[0] % (N_SEQ - first_pieces)
    inner_start = inner_piece * TOK + 1 + chosen[1] % (FILT - 2)
    flags = (jax.random.randint(second_key, (TOKENS,), 0, spacing) == 0) & (positions >= quarter)
    is_start = flags | (positions % quarter == 0) | (positions == inner_start)
    starts = jnp.where(is_start, positions, 0)
    back = positions - lax.cummax(starts, axis=0)
    later = jnp.where(is_start & (positions > 0), positions, TOKENS)
    later_shift = jnp.concatenate([later[1:], jnp.full((1,), TOKENS, jnp.int32)], 0)
    ahead = lax.cummin(later_shift, axis=0, reverse=True) - 1 - positions
    back_stored = back.reshape(N_SEQ, TOK)[pack].reshape(TOKENS)
    ahead_stored = ahead.reshape(N_SEQ, TOK)[pack].reshape(TOKENS)
    return (pack, back_stored, ahead_stored)


def draw_pack(key, part):
    return layout_draw(key)[0]


def draw_since_start(key, part):
    return layout_draw(key)[1]


def draw_until_end(key, part):
    return layout_draw(key)[2]


def draw_long_filter(key, part):
    key = jax.random.fold_in(key, 11)
    rate_key, base_key = jax.random.split(key)
    rates = jnp.exp(jax.random.uniform(rate_key, (1, D), jnp.float32, math.log(0.003), math.log(0.08)))
    base = jax.random.normal(base_key, (FILT, D), jnp.float32)
    taps = jnp.arange(FILT, dtype=jnp.float32)[:, None]
    return (0.15 * base * jnp.exp(-rates * taps)).astype(jnp.float32)


def level_of(rng, shape, cuts, low, top_value):
    def one(position, blocks):
        draws = jax.random.uniform(jax.random.fold_in(jax.random.fold_in(rng, 6), position), (blocks,), jnp.float32, low / len(cuts), top_value / len(cuts))
        return jnp.repeat(jnp.exp(draws), shape[position] // blocks).reshape((-1,) + (1,) * (len(shape) - position - 1))

    loudness = one(*cuts[0])
    for cut in cuts[1:]:
        loudness = loudness * one(*cut)
    return loudness


def normal_values(key, extent, deviation, bound, cuts=(), kind=jnp.bfloat16):
    values = jax.random.normal(key, extent, jnp.float32) * deviation
    if len(cuts) > 0:
        values = level_of(key, extent, cuts, -0.22, 0.18) * values
    return jnp.clip(values, min=-bound, max=bound).astype(kind)


def setup_inputs(seed: int = 0) -> dict:
    arg_keys = jax.random.split(jax.random.key(seed), 9)
    return {
        "proj": normal_values(arg_keys[0], (3, TOKENS, D), 1.0, 6.0, ((1, 16), (2, 16))),
        "short_filters": normal_values(arg_keys[1], (3, SHORT, D), 0.4, 2.4, ((2, 16),), jnp.float32),
        "long_filter": draw_long_filter(jax.random.fold_in(arg_keys[8], 71), 0),
        "out_weight": normal_values(arg_keys[3], (D, D), D ** -0.5, 0.0625, ((0, 16), (1, 16))),
        "cotangent": normal_values(arg_keys[4], (TOKENS, D), 1.0, 6.0, ((0, 16), (1, 16))),
        "pack": draw_pack(jax.random.fold_in(arg_keys[8], 71), 0),
        "since_start": draw_since_start(jax.random.fold_in(arg_keys[8], 71), 0),
        "until_end": draw_until_end(jax.random.fold_in(arg_keys[8], 71), 0),
    }


def filter_taps(extended, weights, reach, tap_count, length, backward):
    def step(index, running):
        begin = index if backward else tap_count - 1 - index
        window = lax.dynamic_slice_in_dim(extended, begin, length, 0).astype(jnp.float32)
        row = lax.dynamic_slice_in_dim(weights, index, 1, 0)
        return running + jnp.where((reach >= index)[:, None], row * window, 0.0)
    return lax.fori_loop(0, tap_count, step, jnp.zeros((length, extended.shape[1]), jnp.float32))


def reference(proj, short_filters, long_filter, out_weight, cotangent, pack, since_start, until_end):
    order = jnp.zeros((N_SEQ,), jnp.int32).at[pack].set(jnp.arange(N_SEQ, dtype=jnp.int32))

    def logical(array):
        blocks = array.reshape((N_SEQ, TOK) + array.shape[1:])
        return blocks[order].reshape(array.shape)

    def stored(array):
        blocks = array.reshape((N_SEQ, TOK) + array.shape[1:])
        return blocks[pack].reshape(array.shape)

    back = logical(since_start)
    ahead = logical(until_end)
    width = proj.shape[2]
    front_short = jnp.zeros((SHORT - 1, width), jnp.bfloat16)
    front_long = jnp.zeros((FILT - 1, width), jnp.bfloat16)
    streams = []
    for which in range(3):
        source = logical(proj[which])
        extended = jnp.concatenate([front_short, source], 0)
        streams.append(filter_taps(extended, short_filters[which], back, SHORT, TOKENS, False).astype(jnp.bfloat16))
    q_short, k_short, v_short = streams
    mixed_u = (k_short.astype(jnp.float32) * v_short.astype(jnp.float32)).astype(jnp.bfloat16)
    long_out = filter_taps(jnp.concatenate([front_long, mixed_u], 0), long_filter, back, FILT, TOKENS, False)
    gated = (q_short.astype(jnp.float32) * long_out).astype(jnp.bfloat16)
    mixed = jnp.dot(gated, out_weight, preferred_element_type=jnp.float32).astype(jnp.bfloat16)
    cot_logical = logical(cotangent)
    grad_gated = jnp.dot(cot_logical, out_weight.T, preferred_element_type=jnp.float32).astype(jnp.bfloat16)
    grad_long = (grad_gated.astype(jnp.float32) * q_short.astype(jnp.float32)).astype(jnp.bfloat16)
    grad_qshort = (grad_gated.astype(jnp.float32) * long_out).astype(jnp.bfloat16)
    grad_mixed = filter_taps(jnp.concatenate([grad_long, front_long], 0), long_filter, ahead, FILT, TOKENS, True)
    grad_kshort = (grad_mixed * v_short.astype(jnp.float32)).astype(jnp.bfloat16)
    grad_vshort = (grad_mixed * k_short.astype(jnp.float32)).astype(jnp.bfloat16)
    grads = []
    for which, source in enumerate([grad_qshort, grad_kshort, grad_vshort]):
        extended = jnp.concatenate([source, front_short], 0)
        grads.append(stored(filter_taps(extended, short_filters[which], ahead, SHORT, TOKENS, True).astype(jnp.bfloat16)))
    return stored(mixed), jnp.stack(grads, 0)
```

```python
import functools

import jax
import jax.numpy as jnp
import numpy as np
from jax import lax
from jax.experimental import pallas as pl
from jax.experimental.pallas import tpu as pltpu
from jax.sharding import PartitionSpec as P

MESH = pl.DeviceIdType.MESH
BF = jnp.bfloat16
F32 = jnp.float32
TOK = 512
CH = 512
FILT = 128
SHORT = 7
MSG = 160
LIMIT = 56 << 20
VM = pltpu.VMEM


def vspec():
    return pl.BlockSpec(memory_space=pltpu.VMEM)


def sspec():
    return pl.BlockSpec(memory_space=pltpu.SMEM)


def dft_tables():
    k = np.arange(128)[:, None] + 0.5
    n = np.arange(256)[None, :]
    angle = 2 * np.pi * k * n / 256
    fwd = np.concatenate([np.cos(angle), -np.sin(angle)], 0)
    inv = np.concatenate([np.cos(angle), -np.sin(angle)], 0).T / 128
    return (
        jnp.asarray(fwd, BF),
        jnp.asarray(inv[128:], BF),
        jnp.asarray(inv[:128], BF),
    )


def bdot(a, b):
    return jnp.dot(a, b, preferred_element_type=F32)


def causal_chunk(x, w_ref, which, lanes, reach, masked):
    total = x[8:72] * w_ref[which, 0:1, lanes]
    for i in range(1, SHORT):
        term = pltpu.roll(x, i, 0)[8:72] * w_ref[which, i : i + 1, lanes]
        if masked:
            term = jnp.where(reach >= i, term, 0.0)
        total = total + term
    return total.astype(BF)


def ahead_chunk(x, w_ref, which, lanes, reach, masked):
    total = x[0:64] * w_ref[which, 0:1, lanes]
    for i in range(1, SHORT):
        term = pltpu.roll(x, 72 - i, 0)[0:64] * w_ref[which, i : i + 1, lanes]
        if masked:
            term = jnp.where(reach >= i, term, 0.0)
        total = total + term
    return total.astype(BF)


def both_ways(is_masked, run):
    @pl.when(is_masked)
    def _():
        run(True)

    @pl.when(jnp.logical_not(is_masked))
    def _():
        run(False)


def tail_kernel(low_ref, proj_ref, w_ref, reach_ref, msg_ref, ext):
    for s in range(3):
        ext[s] = proj_ref[s, 112:256, :].astype(F32)
    for c in range(2):

        def run(masked):
            for g in range(4):
                lanes = pl.ds(g * 128, 128)
                reach = reach_ref[pl.ds(128 + c * 64, 64), :]
                ks = causal_chunk(ext[1, pl.ds(8 + c * 64, 72), lanes], w_ref, 1, lanes, reach, masked)
                vs = causal_chunk(ext[2, pl.ds(8 + c * 64, 72), lanes], w_ref, 2, lanes, reach, masked)
                msg_ref[pl.ds(c * 64, 64), lanes] = (ks.astype(F32) * vs.astype(F32)).astype(BF)

        both_ways(low_ref[6 + c] < SHORT - 1, run)
    msg_ref[128:160, :] = jnp.concatenate(
        [ext[0, 136:144, :], ext[1, 136:144, :], ext[2, 136:144, :], jnp.zeros((8, CH), F32)], 0
    ).astype(BF)


def tail_message(proj, short_filters, reach, low):
    return pl.pallas_call(
        tail_kernel,
        grid=(1,),
        out_shape=jax.ShapeDtypeStruct((MSG, CH), BF),
        in_specs=[
            sspec(),
            pl.BlockSpec((3, 256, CH), lambda i: (0, 1, 0)),
            pl.BlockSpec((3, SHORT, CH), lambda i: (0, 0, 0)),
            pl.BlockSpec((256, 128), lambda i: (1, 0)),
        ],
        out_specs=pl.BlockSpec((MSG, CH), lambda i: (0, 0)),
        scratch_shapes=[VM((3, 144, CH), F32)],
        compiler_params=pltpu.CompilerParams(vmem_limit_bytes=LIMIT),
        name="tail_message",
    )(low, proj, short_filters, reach)


def place():
    s = lax.axis_index("seq")
    c = lax.axis_index("chan")
    return s // 2, s % 2, c // 4, c % 4


def dev(z, k, y, x):
    return (lax.rem(z + 8, 8) * 2 + k, lax.rem(y + 4, 4) * 4 + lax.rem(x + 4, 4))


def greet(targets):
    barrier = pltpu.get_barrier_semaphore()
    for t in targets:
        pl.semaphore_signal(barrier, inc=1, device_id=t, device_id_type=MESH)
    pl.semaphore_wait(barrier, len(targets))


def rcopy(src, dst, ssem, rsem, device):
    return pltpu.make_async_remote_copy(
        src_ref=src, dst_ref=dst, send_sem=ssem, recv_sem=rsem, device_id=device, device_id_type=MESH
    )


class SeqGather:
    def __init__(self, buf, r0, rows, send, recv):
        self.buf, self.r0, self.rows, self.send, self.recv = buf, r0, rows, send, recv
        self.z, self.k, self.y, self.x = place()
        self.sent = []
        self.from_sib = []

    def view(self, z, k, part):
        s = lax.rem(z + 8, 8) * 2 + k
        half = self.rows // 2
        if part == 0:
            return self.buf.at[s, pl.ds(self.r0, self.rows)]
        return self.buf.at[s, pl.ds(self.r0 + (part - 1) * half, half)]

    def ring(self, way, hop):
        v = self.view(self.z - way * (hop - 1), self.k, 0 if hop < 4 else (1 if way > 0 else 2))
        n = (hop - 1) * 2 + (0 if way > 0 else 1)
        return rcopy(v, v, self.send.at[n], self.recv.at[n], dev(self.z + way, self.k, self.y, self.x))

    def landed(self, way, hop):
        v = self.view(self.z - way * hop, self.k, 0 if hop < 4 else (1 if way > 0 else 2))
        n = (hop - 1) * 2 + (0 if way > 0 else 1)
        rcopy(v, v, self.send.at[n], self.recv.at[n], dev(self.z + way, self.k, self.y, self.x)).wait_recv()

    def sib(self, offset, n):
        v = self.view(self.z + offset, self.k, 0)
        copy = rcopy(v, v, self.send.at[8 + n], self.recv.at[8 + n], dev(self.z, 1 - self.k, self.y, self.x))
        copy.start()
        self.sent.append(copy)
        w = self.view(self.z + offset, 1 - self.k, 0)
        self.from_sib.append(
            rcopy(w, w, self.send.at[8 + n], self.recv.at[8 + n], dev(self.z, 1 - self.k, self.y, self.x))
        )

    def go(self, way, hop):
        copy = self.ring(way, hop)
        copy.start()
        self.sent.append(copy)

    def begin(self):
        self.go(1, 1)
        self.go(-1, 1)
        self.sib(0, 0)

    def step(self, hop):
        for way in (1, -1):
            self.landed(way, hop)
            if hop < 4:
                self.go(way, hop + 1)
        if hop < 4:
            self.sib(-hop, 2 * hop - 1)
            self.sib(hop, 2 * hop)
        else:
            self.sib(4, 7)

    def arrived(self):
        for copy in self.from_sib:
            copy.wait_recv()

    def finish(self):
        for copy in self.sent:
            copy.wait_send()


def halo_kernel(msg_ref, all_ref, send, recv, local):
    z, k, y, x = place()
    greet([dev(z + 1, k, y, x), dev(z - 1, k, y, x), dev(z, 1 - k, y, x)])
    own = pltpu.make_async_copy(msg_ref, all_ref.at[z * 2 + k], local)
    own.start()
    own.wait()
    g = SeqGather(all_ref, 0, MSG, send, recv)
    g.begin()
    for hop in range(1, 5):
        g.step(hop)
    g.arrived()
    g.finish()


def halo_gather(msg):
    return pl.pallas_call(
        halo_kernel,
        out_shape=jax.ShapeDtypeStruct((16, MSG, CH), BF),
        in_specs=[vspec()],
        out_specs=vspec(),
        scratch_shapes=[
            pltpu.SemaphoreType.DMA((16,)),
            pltpu.SemaphoreType.DMA((16,)),
            pltpu.SemaphoreType.DMA,
        ],
        compiler_params=pltpu.CompilerParams(
            collective_id=1, has_side_effects=True, vmem_limit_bytes=LIMIT
        ),
        name="halo_gather",
    )(msg)


def forward_kernel(
    from_ref, low_ref, back_ref, ahead_ref, halo_ref, proj_ref, w_ref, long_ref, reach_ref, fwd_ref, inv_ref,
    y_ref, z_ref, qs_ref, ks_ref, vs_ref, spec_ref, ext, u_ext,
):
    h = halo_ref[0]
    u_ext[0:128, :] = h[0:128, :]
    raw = h[128:160, :].astype(F32)
    for s in range(3):
        ext[s, 0:8, :] = raw[s * 8 : s * 8 + 8, :]
        ext[s, 8:520, :] = proj_ref[s].astype(F32)
    spec_ref[...] = bdot(fwd_ref[:, 0:128], long_ref[...].astype(BF))

    @pl.loop(0, 8)
    def _(c):
        start = pl.multiple_of(c * 64, 64)

        def run(masked):
            for g in range(4):
                lanes = pl.ds(g * 128, 128)
                reach = reach_ref[pl.ds(start, 64), :]
                got = [
                    causal_chunk(ext[s, pl.ds(start, 72), lanes], w_ref, s, lanes, reach, masked)
                    for s in range(3)
                ]
                qs_ref[pl.ds(start, 64), lanes] = got[0]
                ks_ref[pl.ds(start, 64), lanes] = got[1]
                vs_ref[pl.ds(start, 64), lanes] = got[2]
                u_ext[pl.ds(start + 128, 64), lanes] = (got[1].astype(F32) * got[2].astype(F32)).astype(BF)

        both_ways(low_ref[c] < SHORT - 1, run)

    rows_in = lax.broadcasted_iota(jnp.int32, (256, 256), 0)
    rows_out = lax.broadcasted_iota(jnp.int32, (128, 256), 0)

    @pl.loop(0, 4)
    def _(b):
        base = pl.multiple_of(b * 128, 128)

        def one(t):
            back, ahead = back_ref[t], ahead_ref[t]
            end = jnp.minimum(t + ahead + 1, base + 128)
            low = t - back - base + 128
            for half in range(2):
                lanes = pl.ds(half * 256, 256)
                x = u_ext[pl.ds(base, 256), lanes].astype(F32)
                x = jnp.where(rows_in >= low, x, 0.0).astype(BF)
                spec = bdot(fwd_ref[...], x)
                xr, xi = spec[0:128], spec[128:256]
                hr, hi = spec_ref[0:128, lanes], spec_ref[128:256, lanes]
                prod = jnp.concatenate([xr * hr - xi * hi, xr * hi + xi * hr], 0).astype(BF)
                out = bdot(inv_ref[...], prod)
                keep = (rows_out >= t - base) & (rows_out < end - base)
                z_ref[pl.ds(base, 128), lanes] = jnp.where(keep, out, z_ref[pl.ds(base, 128), lanes])
            return end

        lax.while_loop(lambda t: t < base + 128, one, base)
        rows = pl.ds(base, 128)
        y_ref[rows, :] = (qs_ref[rows, :].astype(F32) * z_ref[rows, :]).astype(BF)


def forward(prev, low, since, until, halo, proj, short_filters, long_filter, reach, fwd, inv):
    full = lambda *shape: pl.BlockSpec(shape, lambda i, *_: (0,) * len(shape))
    out = jax.ShapeDtypeStruct((TOK, CH), BF)
    return pl.pallas_call(
        forward_kernel,
        grid_spec=pltpu.PrefetchScalarGridSpec(
            num_scalar_prefetch=4,
            grid=(1,),
            in_specs=[
                pl.BlockSpec((1, MSG, CH), lambda i, prev_ref, *_: (prev_ref[0], 0, 0)),
                full(3, TOK, CH),
                full(3, SHORT, CH),
                full(FILT, CH),
                full(TOK, 128),
                full(256, 256),
                full(128, 256),
            ],
            out_specs=[full(TOK, CH)] * 5 + [full(256, CH)],
            scratch_shapes=[VM((3, TOK + 8, CH), F32), VM((TOK + 128, CH), BF)],
        ),
        out_shape=[
            out,
            jax.ShapeDtypeStruct((TOK, CH), F32),
            out,
            out,
            out,
            jax.ShapeDtypeStruct((256, CH), F32),
        ],
        compiler_params=pltpu.CompilerParams(vmem_limit_bytes=LIMIT),
        name="forward_conv",
    )(prev, low, since, until, halo, proj, short_filters, long_filter, reach, fwd, inv)


SUBS = 4
SUBROWS = 512 // SUBS


def product_kernel(
    w_own, cot_own, y_own, z_ref, qs_ref, ks_ref, vs_ref,
    mixed_ref, gy_ref, halo_ref,
    w_all, cot_all, y_all, gy_out, gy_in, mx_out, mx_in,
    local, wsend, wrecv, asend, arecv, gsend, grecv, msend, mrecv, hsend, hrecv,
):
    z, k, y, x = place()
    s_own = z * 2 + k
    greet(
        [
            dev(z + 1, k, y, x), dev(z - 1, k, y, x), dev(z, 1 - k, y, x),
            dev(z, k, y, x + 1), dev(z, k, y, x - 1), dev(z, k, y, x + 2),
            dev(z, k, y + 1, x), dev(z, k, y - 1, x), dev(z, k, y + 2, x),
        ]
    )
    mine = [
        pltpu.make_async_copy(w_own, w_all.at[s_own], local.at[0]),
        pltpu.make_async_copy(cot_own, cot_all.at[y], local.at[1]),
        pltpu.make_async_copy(y_own, y_all.at[x], local.at[2]),
    ]
    for copy in mine:
        copy.start()
    for copy in mine:
        copy.wait()

    sent = []

    def ring4(buf, me, at, base):
        def view(i, part):
            i = lax.rem(i + 4, 4)
            if part == 0:
                return buf.at[i]
            return buf.at[i, pl.ds((part - 1) * 256, 256)]

        def copy(v, n, way):
            return rcopy(v, v, asend.at[base + n], arecv.at[base + n], at(way))

        def begin():
            for n, way in ((0, 1), (1, -1)):
                c = copy(view(me, 0), n, way)
                c.start()
                sent.append(c)

        def forward_on():
            for n, way in ((0, 1), (1, -1)):
                copy(view(me - way, 0), n, way).wait_recv()
                c = copy(view(me - way, 1 + n), 2 + n, way)
                c.start()
                sent.append(c)

        def end():
            for n, way in ((0, 1), (1, -1)):
                copy(view(me + 2, 1 + n), 2 + n, way).wait_recv()

        return begin, forward_on, end

    cot_begin, cot_on, cot_end = ring4(cot_all, y, lambda d: dev(z, k, y + d, x), 0)
    y_begin, y_on, y_end = ring4(y_all, x, lambda d: dev(z, k, y, x + d), 4)

    subs = [SeqGather(w_all, j * SUBROWS, SUBROWS, wsend.at[j], wrecv.at[j]) for j in range(SUBS)]

    def gy_tile(p, a, m):
        rows = pl.ds(m * 256, 256)
        total = jnp.zeros((256, 256), F32)
        for o in range(4):
            total = total + lax.dot_general(
                cot_all[o, rows, :], w_all[4 * o + a, pl.ds(p * 256, 256), :],
                (((1,), (1,)), ((), ())), preferred_element_type=F32,
            )
        gy_out[p, a, rows, :] = total.astype(BF)

    def gy_copy(p, a, m, rel):
        rows = pl.ds(m * 256, 256)
        n = (p * 2 + m) * 3 + rel - 1
        return rcopy(
            gy_out.at[p, a, rows], gy_in.at[p, rel - 1, rows], gsend.at[n], grecv.at[n], dev(z, k, y, a)
        )

    def mixed_part(o):
        @pl.loop(0, 4)
        def _(t):
            rows = pl.ds(pl.multiple_of((t // 2) * 256, 256), 256)
            cols = pl.ds(pl.multiple_of((t % 2) * 256, 256), 256)
            total = jnp.zeros((256, 256), F32)
            for a in range(4):
                total = total + bdot(y_all[a, rows, :], w_all[4 * o + a, :, cols])
            mx_out[o, rows, cols] = total.astype(BF)

    def gy_phase(p, m):
        @pl.loop(0, 4)
        def _(i):
            rel = lax.rem(i + 1, 4)
            a = lax.rem(x + rel, 4)
            gy_tile(p, a, m)

        for rel in (2, 1, 3):
            c = gy_copy(p, lax.rem(x + rel, 4), m, rel)
            c.start()
            sent.append(c)

    cot_begin()
    subs[0].begin()
    subs[1].begin()
    y_begin()
    subs[0].step(1)
    subs[1].step(1)
    subs[0].step(2)
    subs[1].step(2)
    cot_on()
    y_on()
    subs[0].step(3)
    subs[1].step(3)
    subs[2].begin()
    subs[3].begin()
    subs[0].step(4)
    subs[1].step(4)
    subs[0].arrived()
    subs[1].arrived()
    cot_end()
    gy_phase(0, 0)
    subs[2].step(1)
    subs[3].step(1)
    gy_phase(0, 1)
    y_end()
    subs[2].step(2)
    subs[3].step(2)
    subs[2].step(3)
    subs[3].step(3)
    subs[2].step(4)
    subs[3].step(4)
    subs[2].arrived()
    subs[3].arrived()
    gy_phase(1, 0)
    gy_phase(1, 1)

    def mixed_copy(rel):
        o = lax.rem(y + rel, 4)
        return rcopy(mx_out.at[o], mx_in.at[rel - 1], msend.at[rel - 1], mrecv.at[rel - 1], dev(z, k, o, x))

    for rel in (2, 1, 3):
        mixed_part(lax.rem(y + rel, 4))
        c = mixed_copy(rel)
        c.start()
        sent.append(c)

    def gy_sum(m):
        rows = pl.ds(m * 256, 256)
        for p in range(2):
            for rel in (1, 2, 3):
                gy_copy(p, lax.rem(x + rel, 4), m, rel).wait_recv()
            total = gy_out[p, x, rows, :].astype(F32)
            for r in range(3):
                total = total + gy_in[p, r, rows, :].astype(F32)
            gy_ref[rows, p * 256 : p * 256 + 256] = total.astype(BF)

    gy_sum(0)
    head = gy_ref[0:144, :].astype(F32)
    gz = head[0:136] * qs_ref[0:144, :].astype(F32)[0:136]
    gq = head[0:8] * z_ref[0:8, :]
    halo_ref[s_own] = jnp.concatenate(
        [gz, gq, ks_ref[0:16, :].astype(F32)[0:8], vs_ref[0:16, :].astype(F32)[0:8]], 0
    ).astype(BF)
    halo = SeqGather(halo_ref, 0, MSG, hsend, hrecv)
    halo.begin()
    mixed_part(y)
    halo.step(1)
    gy_sum(1)
    halo.step(2)
    halo.step(3)
    halo.step(4)

    for rel in (1, 2, 3):
        mixed_copy(rel).wait_recv()

    @pl.loop(0, 4)
    def _(t):
        rows = pl.ds(pl.multiple_of(t * 128, 128), 128)
        total = mx_out[y, rows, :].astype(F32)
        for r in range(3):
            total = total + mx_in[r, rows, :].astype(F32)
        mixed_ref[rows, :] = total.astype(BF)

    halo.arrived()
    halo.finish()
    for g in subs:
        g.finish()
    for c in sent:
        c.wait_send()


def products(w_own, cot, y, zed, qs, ks, vs):
    out = jax.ShapeDtypeStruct((TOK, CH), BF)
    dma = pltpu.SemaphoreType.DMA
    return pl.pallas_call(
        product_kernel,
        out_shape=[out, out, jax.ShapeDtypeStruct((16, MSG, CH), BF)],
        in_specs=[vspec()] * 7,
        out_specs=[vspec()] * 3,
        scratch_shapes=[
            VM((16, 512, 512), BF),
            VM((4, 512, 512), BF),
            VM((4, 512, 512), BF),
            VM((2, 4, 512, 256), BF),
            VM((2, 3, 512, 256), BF),
            VM((4, 512, 512), BF),
            VM((3, 512, 512), BF),
            dma((3,)),
            dma((SUBS, 16)),
            dma((SUBS, 16)),
            dma((8,)),
            dma((8,)),
            dma((12,)),
            dma((12,)),
            dma((3,)),
            dma((3,)),
            dma((16,)),
            dma((16,)),
        ],
        compiler_params=pltpu.CompilerParams(
            collective_id=2, has_side_effects=True, vmem_limit_bytes=LIMIT
        ),
        name="products",
    )(w_own, cot, y, zed, qs, ks, vs)


def backward_kernel(
    next_ref, low_ref, ahead_ref, halo_ref, gy_ref, z_ref, qs_ref, ks_ref, vs_ref, spec_ref, w_ref, reach_ref,
    fwd_ref, inv_ref,
    grad_ref, gz_ext, g_ext, k_ext, v_ext,
):
    h = halo_ref[0].astype(F32)
    gz_ext[512:656, :] = h[0:144, :].astype(BF)
    gz_ext[656:768, :] = jnp.zeros((112, CH), BF)
    g_ext[0, 512:520, :] = h[136:144, :]
    k_ext[512:528, :] = jnp.concatenate([h[144:152], jnp.zeros((8, CH), F32)], 0).astype(BF)
    v_ext[512:528, :] = jnp.concatenate([h[152:160], jnp.zeros((8, CH), F32)], 0).astype(BF)

    @pl.loop(0, 8)
    def _(c):
        rows = pl.ds(pl.multiple_of(c * 64, 64), 64)
        gy = gy_ref[rows, :].astype(F32)
        gz_ext[rows, :] = (gy * qs_ref[rows, :].astype(F32)).astype(BF)
        g_ext[0, rows, :] = (gy * z_ref[rows, :]).astype(BF).astype(F32)

    rows_in = lax.broadcasted_iota(jnp.int32, (256, 256), 0)
    rows_out = lax.broadcasted_iota(jnp.int32, (128, 256), 0)

    def correlate(base, high, lanes, count):
        x = gz_ext[pl.ds(base, 256), lanes].astype(F32)
        x = jnp.where(rows_in < high, x, 0.0).astype(BF)
        spec = bdot(fwd_ref[...], x)
        xr, xi = spec[0:128], spec[128:256]
        hr, hi = spec_ref[0:128, lanes], spec_ref[128:256, lanes]
        prod = jnp.concatenate([xr * hr + xi * hi, xi * hr - xr * hi], 0).astype(BF)
        return bdot(inv_ref[0:count, :], prod)

    @pl.loop(0, 4)
    def _(b):
        base = pl.multiple_of(b * 128, 128)
        rows = pl.ds(base, 128)

        def one(t):
            stop = t + ahead_ref[t] + 1
            end = jnp.minimum(stop, base + 128)
            for half in range(2):
                lanes = pl.ds(half * 256, 256)
                out = correlate(base, stop - base, lanes, 128)
                keep = (rows_out >= t - base) & (rows_out < end - base)
                g_ext[1, rows, lanes] = jnp.where(keep, out, g_ext[1, rows, lanes])
            return end

        lax.while_loop(lambda t: t < base + 128, one, base)
        gu = g_ext[1, rows, :]
        g_ext[1, rows, :] = (gu * vs_ref[rows, :].astype(F32)).astype(BF).astype(F32)
        g_ext[2, rows, :] = (gu * ks_ref[rows, :].astype(F32)).astype(BF).astype(F32)

    for half in range(2):
        lanes = pl.ds(half * 256, 256)
        gu = correlate(512, ahead_ref[511], lanes, 16)
        g_ext[1, 512:520, lanes] = (gu * v_ext[512:528, lanes].astype(F32)).astype(BF).astype(F32)[0:8]
        g_ext[2, 512:520, lanes] = (gu * k_ext[512:528, lanes].astype(F32)).astype(BF).astype(F32)[0:8]

    @pl.loop(0, 8)
    def _(c):
        start = pl.multiple_of(c * 64, 64)

        def run(masked):
            for g in range(4):
                lanes = pl.ds(g * 128, 128)
                reach = reach_ref[pl.ds(start, 64), :]
                for s in range(3):
                    grad_ref[s, pl.ds(start, 64), lanes] = ahead_chunk(
                        g_ext[s, pl.ds(start, 72), lanes], w_ref, s, lanes, reach, masked
                    )

        both_ways(low_ref[c] < SHORT - 1, run)


def backward(nxt, low, until, halo, gy, zed, qs, ks, vs, spec, short_filters, reach, fwd, inv):
    full = lambda *shape: pl.BlockSpec(shape, lambda i, *_: (0,) * len(shape))
    return pl.pallas_call(
        backward_kernel,
        grid_spec=pltpu.PrefetchScalarGridSpec(
            num_scalar_prefetch=3,
            grid=(1,),
            in_specs=[
                pl.BlockSpec((1, MSG, CH), lambda i, next_ref, *_: (next_ref[0], 0, 0)),
                full(TOK, CH),
                full(TOK, CH),
                full(TOK, CH),
                full(TOK, CH),
                full(TOK, CH),
                full(256, CH),
                full(3, SHORT, CH),
                full(TOK, 128),
                full(256, 256),
                full(128, 256),
            ],
            out_specs=full(3, TOK, CH),
            scratch_shapes=[
                VM((768, CH), BF),
                VM((3, TOK + 8, CH), F32),
                VM((TOK + 16, CH), BF),
                VM((TOK + 16, CH), BF),
            ],
        ),
        out_shape=jax.ShapeDtypeStruct((3, TOK, CH), BF),
        compiler_params=pltpu.CompilerParams(vmem_limit_bytes=LIMIT),
        name="backward_conv",
    )(nxt, low, until, halo, gy, zed, qs, ks, vs, spec, short_filters, reach, fwd, inv)


def weight_pairs():
    pairs = []
    for seq in range(16):
        for chan in range(16):
            m, a, y, b = seq // 4, seq % 4, chan // 4, chan % 4
            pairs.append((seq * 16 + chan, (4 * m + b) * 16 + 4 * y + a))
    return pairs


def body(proj, short_filters, long_filter, out_weight, cotangent, pack, since_start, until_end):
    fwd, inv_last, inv_first = dft_tables()
    w_own = lax.ppermute(out_weight, ("seq", "chan"), weight_pairs())
    own_piece = pack[lax.axis_index("seq")]
    place_of = jnp.arange(16, dtype=jnp.int32)
    prev = jnp.sum(jnp.where(pack == own_piece - 1, place_of, 0)).reshape(1)
    nxt = jnp.sum(jnp.where(pack == own_piece + 1, place_of, 0)).reshape(1)
    back = jnp.broadcast_to(since_start[:, None], (TOK, 128))
    ahead = jnp.broadcast_to(until_end[:, None], (TOK, 128))
    back_low = jnp.min(since_start.reshape(8, 64), axis=1)
    ahead_low = jnp.min(until_end.reshape(8, 64), axis=1)

    msg = tail_message(proj, short_filters, back, back_low)
    halo = halo_gather(msg)
    y, zed, qs, ks, vs, spec = forward(
        prev, back_low, since_start, until_end, halo, proj, short_filters, long_filter, back, fwd, inv_last
    )
    mixed, gy, halo_next = products(w_own, cotangent, y, zed, qs, ks, vs)
    grad = backward(
        nxt, ahead_low, until_end, halo_next, gy, zed, qs, ks, vs, spec, short_filters, ahead, fwd, inv_first
    )
    return (mixed, grad)


def solution(mesh):
    return jax.shard_map(
        body,
        mesh=mesh,
        in_specs=(
            P(None, "seq", "chan"),
            P(None, None, "chan"),
            P(None, "chan"),
            P("chan", "seq"),
            P("seq", "chan"),
            P(),
            P("seq"),
            P("seq"),
        ),
        out_specs=(P("seq", "chan"), P(None, "seq", "chan")),
        check_vma=False,
    )
```

```python
import functools

import jax
import jax.numpy as jnp
import numpy as np
from jax import lax
from jax.experimental import pallas as pl
from jax.experimental.pallas import tpu as pltpu
from jax.sharding import PartitionSpec as P

MESH = pl.DeviceIdType.MESH
BF = jnp.bfloat16
F32 = jnp.float32
TOK = 512
CH = 512
FILT = 128
SHORT = 7
MSG = 160
LIMIT = 56 << 20
VM = pltpu.VMEM


def vspec():
    return pl.BlockSpec(memory_space=pltpu.VMEM)


def sspec():
    return pl.BlockSpec(memory_space=pltpu.SMEM)


def dft_tables():
    k = np.arange(128)[:, None] + 0.5
    n = np.arange(256)[None, :]
    angle = 2 * np.pi * k * n / 256
    fwd = np.concatenate([np.cos(angle), -np.sin(angle)], 0)
    inv = np.concatenate([np.cos(angle), -np.sin(angle)], 0).T / 128
    return (
        jnp.asarray(fwd, BF),
        jnp.asarray(inv[128:], BF),
        jnp.asarray(inv[:128], BF),
    )


LEVELS = (64, 32, 16, 8)


def level_tables():
    fwd, inv, taps = [], [], []
    for run in LEVELS:
        pair = 2 * run
        k = np.arange(run)[:, None] + 0.5
        n = np.arange(pair)[None, :]
        angle = 2 * np.pi * k * n / pair
        cos, sin = np.cos(angle), np.sin(angle)
        first = (n < run).astype(np.float64)
        pairs = np.eye(256 // pair)
        fwd.append(np.concatenate([np.kron(pairs, cos * first), np.kron(pairs, -sin * first)], 0))
        last = 1.0 - first
        inv.append(
            np.concatenate([np.kron(pairs, cos * last), np.kron(pairs, -sin * last)], 0).T / run
        )
        wide = np.zeros((run, FILT))
        re, im = wide.copy(), wide.copy()
        re[:, :pair], im[:, :pair] = cos, -sin
        taps.append(np.concatenate([np.tile(re, (128 // run, 1)), np.tile(im, (128 // run, 1))], 0))
    return tuple(jnp.asarray(np.stack(t), BF) for t in (fwd, inv, taps))


def bdot(a, b):
    return jnp.dot(a, b, preferred_element_type=F32)


def reach_rows(row_ref, group):
    line = jnp.broadcast_to(row_ref[pl.ds(group, 1), :], (128, 128))
    return jnp.transpose(line.astype(F32))


def causal_chunk(ext, which, start, w_ref, g, reach):
    lanes = pl.ds(g * 128, 128)
    total = ext[which * 4 + g, pl.ds(start + 8, 64), :] * w_ref[which, 0:1, lanes]
    for i in range(1, SHORT):
        term = ext[which * 4 + g, pl.ds(start + 8 - i, 64), :] * w_ref[which, i : i + 1, lanes]
        if reach is not None:
            term = jnp.where(reach >= i, term, 0.0)
        total = total + term
    return total.astype(BF)


def ahead_chunk(ext, which, start, w_ref, g, reach):
    lanes = pl.ds(g * 128, 128)
    total = ext[which * 4 + g, pl.ds(start, 64), :] * w_ref[which, 0:1, lanes]
    for i in range(1, SHORT):
        term = ext[which * 4 + g, pl.ds(start + i, 64), :] * w_ref[which, i : i + 1, lanes]
        if reach is not None:
            term = jnp.where(reach >= i, term, 0.0)
        total = total + term
    return total.astype(BF)


def both_ways(is_masked, row_ref, group, half, reach, run):
    @pl.when(is_masked)
    def _():
        reach[...] = reach_rows(row_ref, group)
        run(reach[pl.ds(pl.multiple_of(half * 64, 64), 64), :])

    @pl.when(jnp.logical_not(is_masked))
    def _():
        run(None)


def causal_masked(back_ref, ahead_ref, first):
    return (back_ref[first] < SHORT - 1) | (ahead_ref[first] < 63)


def ahead_masked(back_ref, ahead_ref, first):
    return (ahead_ref[first + 63] < SHORT - 1) | (back_ref[first + 63] < 63)


def tail_kernel(back_ref, ahead_ref, proj_ref, w_ref, row_ref, msg_ref, ext, reach):
    for s in range(3):
        for g in range(4):
            ext[s * 4 + g] = proj_ref[s, 112:256, pl.ds(g * 128, 128)].astype(F32)
    for c in range(2):

        def run(reach):
            for g in range(4):
                lanes = pl.ds(g * 128, 128)
                ks = causal_chunk(ext, 1, 8 + c * 64, w_ref, g, reach)
                vs = causal_chunk(ext, 2, 8 + c * 64, w_ref, g, reach)
                msg_ref[pl.ds(c * 64, 64), lanes] = (ks.astype(F32) * vs.astype(F32)).astype(BF)

        both_ways(causal_masked(back_ref, ahead_ref, 384 + c * 64), row_ref, 3, c, reach, run)
    for g in range(4):
        msg_ref[128:160, pl.ds(g * 128, 128)] = jnp.concatenate(
            [ext[s * 4 + g, 136:144, :] for s in range(3)] + [jnp.zeros((8, 128), F32)], 0
        ).astype(BF)


def tail_message(since, until, proj, short_filters, rows):
    return pl.pallas_call(
        tail_kernel,
        grid=(1,),
        out_shape=jax.ShapeDtypeStruct((MSG, CH), BF),
        in_specs=[
            sspec(),
            sspec(),
            pl.BlockSpec((3, 256, CH), lambda i: (0, 1, 0)),
            pl.BlockSpec((3, SHORT, CH), lambda i: (0, 0, 0)),
            pl.BlockSpec((4, 128), lambda i: (0, 0)),
        ],
        out_specs=pl.BlockSpec((MSG, CH), lambda i: (0, 0)),
        scratch_shapes=[VM((12, 144, 128), F32), VM((128, 128), F32)],
        compiler_params=pltpu.CompilerParams(vmem_limit_bytes=LIMIT),
        name="tail_message",
    )(since, until, proj, short_filters, rows)


def place():
    s = lax.axis_index("seq")
    c = lax.axis_index("chan")
    return s // 2, s % 2, c // 4, c % 4


def dev(z, k, y, x):
    return (lax.rem(z + 8, 8) * 2 + k, lax.rem(y + 4, 4) * 4 + lax.rem(x + 4, 4))


def greet(targets):
    barrier = pltpu.get_barrier_semaphore()
    for t in targets:
        pl.semaphore_signal(barrier, inc=1, device_id=t, device_id_type=MESH)
    pl.semaphore_wait(barrier, len(targets))


def rcopy(src, dst, ssem, rsem, device):
    return pltpu.make_async_remote_copy(
        src_ref=src, dst_ref=dst, send_sem=ssem, recv_sem=rsem, device_id=device, device_id_type=MESH
    )


class SeqGather:
    def __init__(self, buf, r0, rows, send, recv):
        self.buf, self.r0, self.rows, self.send, self.recv = buf, r0, rows, send, recv
        self.z, self.k, self.y, self.x = place()
        self.sent = []
        self.from_sib = []
        self.seen = 0

    def view(self, z, k, part):
        s = lax.rem(z + 8, 8) * 2 + k
        half = self.rows // 2
        if part == 0:
            return self.buf.at[s, pl.ds(self.r0, self.rows)]
        return self.buf.at[s, pl.ds(self.r0 + (part - 1) * half, half)]

    def ring(self, way, hop):
        v = self.view(self.z - way * (hop - 1), self.k, 0 if hop < 4 else (1 if way > 0 else 2))
        n = (hop - 1) * 2 + (0 if way > 0 else 1)
        return rcopy(v, v, self.send.at[n], self.recv.at[n], dev(self.z + way, self.k, self.y, self.x))

    def landed(self, way, hop):
        v = self.view(self.z - way * hop, self.k, 0 if hop < 4 else (1 if way > 0 else 2))
        n = (hop - 1) * 2 + (0 if way > 0 else 1)
        rcopy(v, v, self.send.at[n], self.recv.at[n], dev(self.z + way, self.k, self.y, self.x)).wait_recv()

    def sib(self, offset, n):
        v = self.view(self.z + offset, self.k, 0)
        copy = rcopy(v, v, self.send.at[8 + n], self.recv.at[8 + n], dev(self.z, 1 - self.k, self.y, self.x))
        copy.start()
        self.sent.append(copy)
        w = self.view(self.z + offset, 1 - self.k, 0)
        self.from_sib.append(
            rcopy(w, w, self.send.at[8 + n], self.recv.at[8 + n], dev(self.z, 1 - self.k, self.y, self.x))
        )

    def go(self, way, hop):
        copy = self.ring(way, hop)
        copy.start()
        self.sent.append(copy)

    def begin(self):
        self.go(1, 1)
        self.go(-1, 1)
        self.sib(0, 0)

    def step(self, hop):
        for way in (1, -1):
            self.landed(way, hop)
            if hop < 4:
                self.go(way, hop + 1)
        if hop < 4:
            self.sib(-hop, 2 * hop - 1)
            self.sib(hop, 2 * hop)
        else:
            self.sib(4, 7)

    def arrived(self, count=8):
        while self.seen < count:
            self.from_sib[self.seen].wait_recv()
            self.seen += 1

    def finish(self):
        for copy in self.sent:
            copy.wait_send()


HALO_SUBS = ((0, 64), (64, 64), (128, 32))


def halo_gathers(buf, send, recv):
    return [SeqGather(buf, r0, rows, send.at[j], recv.at[j]) for j, (r0, rows) in enumerate(HALO_SUBS)]


def holder(pack_ref, seq, shift):
    wanted = pack_ref[seq] + shift
    found = jnp.int32(0)
    for i in range(16):
        found = found + jnp.where(pack_ref[i] == wanted, i, 0)
    return found


SUBS = 4
SUBROWS = 512 // SUBS
TILES = (pl.ds(0, 160), pl.ds(160, 352))


def product_kernel(
    pack_ref, msg_ref, w_ref, cot_own, proj_ref, short_ref, long_ref, back_row, ahead_row,
    table_ref, inv_ref, lfwd_ref, linv_ref, ltaps_ref,
    mixed_ref, gy_ref, next_ref, z_ref, qs_ref, ks_ref, vs_ref, spec_ref,
    halo_ref, w_all, cot_all, y_all, gy_out, gy_in, mx_out, mx_in, ext, u_ext, back_b, ahead_b,
    local, swap, wsend, wrecv, asend, arecv, gsend, grecv, msend, mrecv, hsend, hrecv,
):
    z, k, y, x = place()
    s_own = z * 2 + k
    turn = lax.rem(s_own, 4)
    partner = (s_own - turn + x, 4 * y + turn)
    mine = [
        pltpu.make_async_copy(msg_ref, halo_ref.at[0, s_own], local.at[0]),
        pltpu.make_async_copy(cot_own, cot_all.at[y], local.at[1]),
    ]
    for copy in mine:
        copy.start()
    barrier = pltpu.get_barrier_semaphore()
    for t in (
        dev(z + 1, k, y, x), dev(z - 1, k, y, x), dev(z, 1 - k, y, x),
        dev(z, k, y, x + 1), dev(z, k, y, x - 1), dev(z, k, y, x + 2),
        dev(z, k, y + 1, x), dev(z, k, y - 1, x), dev(z, k, y + 2, x),
    ):
        pl.semaphore_signal(barrier, inc=1, device_id=t, device_id_type=MESH)

    @pl.when(turn != x)
    def _():
        pl.semaphore_signal(barrier, inc=1, device_id=partner, device_id_type=MESH)
        pl.semaphore_wait(barrier, 10)

    @pl.when(turn == x)
    def _():
        pl.semaphore_wait(barrier, 9)

    for copy in mine:
        copy.wait()

    sent = []

    def ring4(buf, me, at, base, r0, rows):
        def view(i, part):
            i = lax.rem(i + 4, 4)
            if part == 0:
                return buf.at[i, pl.ds(r0, rows)]
            return buf.at[i, pl.ds(r0 + (part - 1) * (rows // 2), rows // 2)]

        def copy(v, n, way):
            return rcopy(v, v, asend.at[base + n], arecv.at[base + n], at(way))

        def begin():
            for n, way in ((0, 1), (1, -1)):
                c = copy(view(me, 0), n, way)
                c.start()
                sent.append(c)

        def forward_on():
            for n, way in ((0, 1), (1, -1)):
                copy(view(me - way, 0), n, way).wait_recv()
                c = copy(view(me - way, 1 + n), 2 + n, way)
                c.start()
                sent.append(c)

        def end():
            for n, way in ((0, 1), (1, -1)):
                copy(view(me + 2, 1 + n), 2 + n, way).wait_recv()

        return begin, forward_on, end

    cot_begin, cot_on, cot_end = ring4(cot_all, y, lambda d: dev(z, k, y + d, x), 0, 0, 512)
    y_ring = [ring4(y_all, x, lambda d: dev(z, k, y, x + d), 4 + 4 * n, 256 * n, 256) for n in range(2)]

    subs = [SeqGather(w_all, j * SUBROWS, SUBROWS, wsend.at[j], wrecv.at[j]) for j in range(SUBS)]

    def gy_tile(p, a, m):
        rows = TILES[m]
        total = jnp.zeros((rows.size, 256), F32)
        for o in range(4):
            total = total + lax.dot_general(
                cot_all[o, rows, :], w_all[4 * o + a, pl.ds(p * 256, 256), :],
                (((1,), (1,)), ((), ())), preferred_element_type=F32,
            )
        gy_out[p, a, rows, :] = total.astype(BF)

    def gy_copy(p, a, m, rel):
        rows = TILES[m]
        n = (p * 2 + m) * 3 + rel - 1
        return rcopy(
            gy_out.at[p, a, rows], gy_in.at[p, rel - 1, rows], gsend.at[n], grecv.at[n], dev(z, k, y, a)
        )

    def mixed_part(o):
        @pl.loop(0, 4)
        def _(t):
            rows = pl.ds(pl.multiple_of((t // 2) * 256, 256), 256)
            cols = pl.ds(pl.multiple_of((t % 2) * 256, 256), 256)
            total = jnp.zeros((256, 256), F32)
            for a in range(4):
                total = total + bdot(y_all[a, rows, :], w_all[4 * o + a, :, cols])
            mx_out[o, rows, cols] = total.astype(BF)

    def gy_phase(p, m):
        @pl.loop(0, 4)
        def _(i):
            rel = lax.rem(i + 1, 4)
            a = lax.rem(x + rel, 4)
            gy_tile(p, a, m)

        for rel in (2, 1, 3):
            c = gy_copy(p, lax.rem(x + rel, 4), m, rel)
            c.start()
            sent.append(c)

    def short_chunk(c):
        start = c * 64
        reach = back_b[start : start + 64, :]
        for g in range(4):
            lanes = pl.ds(g * 128, 128)
            got = [causal_chunk(ext, s, start, short_ref, g, reach) for s in range(3)]
            qs_ref[pl.ds(start, 64), lanes] = got[0]
            ks_ref[pl.ds(start, 64), lanes] = got[1]
            vs_ref[pl.ds(start, 64), lanes] = got[2]
            u_ext[g, pl.ds(start + 8, 64), :] = (got[1].astype(F32) * got[2].astype(F32)).astype(BF).astype(F32)

    def near_chunk(c):
        start = c * 64
        inside = lax.broadcasted_iota(jnp.int32, (64, 128), 0) % 8
        reach = jnp.minimum(back_b[start : start + 64, :], inside.astype(F32))
        for g in range(4):
            lanes = pl.ds(g * 128, 128)
            total = u_ext[g, pl.ds(start + 8, 64), :] * long_ref[0:1, lanes]
            for i in range(1, 8):
                term = u_ext[g, pl.ds(start + 8 - i, 64), :] * long_ref[i : i + 1, lanes]
                total = total + jnp.where(reach >= i, term, 0.0)
            z_ref[pl.ds(start, 64), lanes] = total

    def wide(mask):
        return jnp.concatenate([mask] * 2, axis=1)

    def times(spec, filt):
        n = spec.shape[0] // 2
        xr, xi, hr, hi = spec[:n], spec[n:], filt[:n], filt[n:]
        return jnp.concatenate([xr * hr - xi * hi, xr * hi + xi * hr], 0).astype(BF)

    def pairs_of_runs(batch):
        rows = pl.ds(batch * 256, 256)
        pos = lax.broadcasted_iota(jnp.int32, (256, 128), 0)

        @pl.loop(0, 4)
        def _(n):
            run = jnp.int32(64) >> n
            at = pos & (run - 1)
            second = (pos & run) != 0
            left = run - at
            into = jnp.where(
                jnp.logical_not(second) & (ahead_b[rows, :] >= left.astype(F32)), 1.0, 0.0
            )
            out = jnp.where(second & (back_b[rows, :] > at.astype(F32)), 1.0, 0.0)
            taps = bdot(ltaps_ref[n], long_ref[...].astype(BF))
            for half in range(2):
                lanes = pl.ds(half * 256, 256)
                u = jnp.concatenate(
                    [u_ext[half * 2 + g, pl.ds(batch * 256 + 8, 256), :] * into for g in range(2)], axis=1
                ).astype(BF)
                spec = bdot(lfwd_ref[n], u)
                prod = times(spec, taps[:, half * 256 : half * 256 + 256])
                z_ref[rows, lanes] += bdot(linv_ref[n], prod) * wide(out)

    def across(block, before):
        rows = pl.ds(block * 128, 128)
        pos = lax.broadcasted_iota(jnp.int32, (128, 128), 0)
        out = jnp.where(back_b[rows, :] > pos.astype(F32), 1.0, 0.0)
        for half in range(2):
            lanes = pl.ds(half * 256, 256)
            spec = bdot(table_ref[:, 0:128], before(half))
            prod = times(spec, spec_ref[:, lanes])
            z_ref[rows, lanes] += bdot(inv_ref[...], prod) * wide(out)

    def own_before(block):
        def get(half):
            pos = lax.broadcasted_iota(jnp.int32, (128, 128), 0)
            left = (128 - pos).astype(F32)
            into = jnp.where(ahead_b[pl.ds((block - 1) * 128, 128), :] >= left, 1.0, 0.0)
            return jnp.concatenate(
                [u_ext[half * 2 + g, pl.ds((block - 1) * 128 + 8, 128), :] * into for g in range(2)], axis=1
            ).astype(BF)

        return get

    def halo_before(half):
        pos = lax.broadcasted_iota(jnp.int32, (128, 128), 0)
        into = jnp.where(back_b[0:1, :] >= (128 - pos).astype(F32), 1.0, 0.0)
        return (got[0:128, half * 256 : half * 256 + 256].astype(F32) * wide(into)).astype(BF)

    def finish_y(batch):
        rows = pl.ds(batch * 256, 256)
        y_all[x, rows, :] = (qs_ref[rows, :].astype(F32) * z_ref[rows, :]).astype(BF)

    early = halo_gathers(halo_ref.at[0], hsend.at[0], hrecv.at[0])
    for g in early:
        g.begin()
    keep = pltpu.make_async_copy(w_ref, w_all.at[s_own], local.at[2])

    def swap_part(j, to):
        rows = pl.ds(j * SUBROWS, SUBROWS)
        return rcopy(w_ref.at[rows], w_all.at[to, rows], swap.at[0, j], swap.at[1, j], partner)

    @pl.when(turn != x)
    def _():
        for j in range(SUBS):
            swap_part(j, partner[0]).start()

    @pl.when(turn == x)
    def _():
        keep.start()
        keep.wait()

    def swapped(j):
        @pl.when(turn != x)
        def _():
            swap_part(j, s_own).wait_recv()
            swap_part(j, partner[0]).wait_send()

    cot_begin()
    for g in range(4):
        back_b[g * 128 : g * 128 + 128, :] = reach_rows(back_row, g)
        ahead_b[g * 128 : g * 128 + 128, :] = reach_rows(ahead_row, g)
    for s in range(3):
        for g in range(4):
            ext[s * 4 + g, 8:520, :] = proj_ref[s, :, pl.ds(g * 128, 128)].astype(F32)
    def hop(group, n):
        for g in group:
            g.step(n)

    first, second = subs[:2], subs[2:]
    for c in (7, 6):
        short_chunk(c)
    hop(early, 1)
    for c in (5, 4):
        short_chunk(c)
    spec_ref[...] = bdot(table_ref[:, 0:128], long_ref[...].astype(BF))
    hop(early, 2)
    for c in (3, 2, 1):
        short_chunk(c)
    hop(early, 3)
    for c in range(4, 8):
        near_chunk(c)
    pairs_of_runs(1)
    hop(early, 4)
    across(2, own_before(2))
    across(3, own_before(3))
    finish_y(1)
    y_ring[1][0]()
    for j in range(2):
        swapped(j)
        subs[j].begin()
    for g in early:
        g.arrived()
    got = halo_ref[0, holder(pack_ref, s_own, -1)]
    raw = got[128:160, :].astype(F32)
    for s in range(3):
        for g in range(4):
            ext[s * 4 + g, 0:8, :] = raw[s * 8 : s * 8 + 8, g * 128 : g * 128 + 128]
    short_chunk(0)
    cot_on()
    for c in range(4):
        near_chunk(c)
    pairs_of_runs(0)
    hop(first, 1)
    across(0, halo_before)
    across(1, own_before(1))
    finish_y(0)
    y_ring[0][0]()
    hop(first, 2)
    hop(first, 3)
    for j in range(2, 4):
        swapped(j)
        subs[j].begin()
    y_ring[1][1]()
    hop(first, 4)
    for g in first:
        g.arrived()
    cot_end()
    gy_phase(0, 0)
    y_ring[0][1]()
    hop(second, 1)
    gy_phase(0, 1)
    y_ring[1][2]()
    y_ring[0][2]()

    def mixed_copy(rel):
        o = lax.rem(y + rel, 4)
        slot = jnp.maximum(rel - 1, 0)
        return rcopy(mx_out.at[o], mx_in.at[slot], msend.at[slot], mrecv.at[slot], dev(z, k, o, x))

    def mixed_send(o):
        mixed_part(o)
        rel = lax.rem(o - y + 4, 4)

        @pl.when(rel != 0)
        def _():
            mixed_copy(rel).start()

    centre = z // 2
    for g in second:
        g.arrived(3)
    mixed_send(centre)
    hop(second, 2)
    hop(second, 3)
    for g in second:
        g.arrived(7)
    mixed_send(lax.rem(centre + 1, 4))
    mixed_send(lax.rem(centre + 3, 4))
    hop(second, 4)
    for g in second:
        g.arrived()
    gy_phase(1, 0)
    mixed_send(lax.rem(centre + 2, 4))

    def gy_sum(m):
        rows = TILES[m]
        for p in range(2):
            for rel in (1, 2, 3):
                gy_copy(p, lax.rem(x + rel, 4), m, rel).wait_recv()
            total = gy_out[p, x, rows, :].astype(F32)
            for r in range(3):
                total = total + gy_in[p, r, rows, :].astype(F32)
            gy_ref[rows, p * 256 : p * 256 + 256] = total.astype(BF)

    gy_sum(0)
    head = gy_ref[0:144, :].astype(F32)
    gz = head[0:136] * qs_ref[0:144, :].astype(F32)[0:136]
    gq = head[0:8] * z_ref[0:8, :]
    halo_ref[1, s_own] = jnp.concatenate(
        [gz, gq, ks_ref[0:16, :].astype(F32)[0:8], vs_ref[0:16, :].astype(F32)[0:8]], 0
    ).astype(BF)
    parts = halo_gathers(halo_ref.at[1], hsend.at[1], hrecv.at[1])
    for g in parts:
        g.begin()
    gy_phase(1, 1)
    for n in (1, 2, 3):
        hop(parts, n)
    gy_sum(1)
    hop(parts, 4)

    for rel in (1, 2, 3):
        mixed_copy(jnp.int32(rel)).wait_recv()
        mixed_copy(jnp.int32(rel)).wait_send()

    @pl.loop(0, 4)
    def _(t):
        rows = pl.ds(pl.multiple_of(t * 128, 128), 128)
        total = mx_out[y, rows, :].astype(F32)
        for r in range(3):
            total = total + mx_in[r, rows, :].astype(F32)
        mixed_ref[rows, :] = total.astype(BF)

    for g in parts:
        g.arrived()
    next_ref[...] = halo_ref[1, holder(pack_ref, s_own, 1)]
    for g in parts:
        g.finish()
    for g in early + subs:
        g.finish()
    for c in sent:
        c.wait_send()


def products(*args):
    out = jax.ShapeDtypeStruct((TOK, CH), BF)
    dma = pltpu.SemaphoreType.DMA
    return pl.pallas_call(
        product_kernel,
        out_shape=[
            out,
            out,
            jax.ShapeDtypeStruct((MSG, CH), BF),
            jax.ShapeDtypeStruct((TOK, CH), F32),
            out,
            out,
            out,
            jax.ShapeDtypeStruct((256, CH), F32),
        ],
        in_specs=[sspec()] + [vspec()] * 13,
        out_specs=[vspec()] * 8,
        scratch_shapes=[
            VM((2, 16, MSG, CH), BF),
            VM((16, 512, 512), BF),
            VM((4, 512, 512), BF),
            VM((4, 512, 512), BF),
            VM((2, 4, 512, 256), BF),
            VM((2, 3, 512, 256), BF),
            VM((4, 512, 512), BF),
            VM((3, 512, 512), BF),
            VM((12, TOK + 8, 128), F32),
            VM((4, TOK + 8, 128), F32),
            VM((TOK, 128), F32),
            VM((TOK, 128), F32),
            dma((3,)),
            dma((2, SUBS)),
            dma((SUBS, 16)),
            dma((SUBS, 16)),
            dma((12,)),
            dma((12,)),
            dma((12,)),
            dma((12,)),
            dma((3,)),
            dma((3,)),
            dma((2, 3, 16)),
            dma((2, 3, 16)),
        ],
        compiler_params=pltpu.CompilerParams(
            collective_id=2, has_side_effects=True, vmem_limit_bytes=LIMIT
        ),
        name="products",
    )(*args)


def backward_kernel(
    back_ref, ahead_ref, halo_ref, gy_ref, z_ref, qs_ref, ks_ref, vs_ref, spec_ref, w_ref, row_ref,
    fwd_ref, inv_ref,
    grad_ref, gz_ext, g_ext, gu, reach,
):
    h = halo_ref[...].astype(F32)
    gz_ext[512:656, :] = h[0:144, :].astype(BF)
    gz_ext[656:768, :] = jnp.zeros((112, CH), BF)
    for g in range(4):
        g_ext[g, 512:520, :] = h[136:144, g * 128 : g * 128 + 128]

    @pl.loop(0, 8)
    def _(c):
        rows = pl.ds(pl.multiple_of(c * 64, 64), 64)
        gy = gy_ref[rows, :].astype(F32)
        gz_ext[rows, :] = (gy * qs_ref[rows, :].astype(F32)).astype(BF)
        gq = (gy * z_ref[rows, :]).astype(BF).astype(F32)
        for g in range(4):
            g_ext[g, rows, :] = gq[:, g * 128 : g * 128 + 128]

    rows_in = lax.broadcasted_iota(jnp.int32, (256, 256), 0)
    rows_out = lax.broadcasted_iota(jnp.int32, (128, 256), 0)

    def correlate(base, high, lanes, count):
        x = gz_ext[pl.ds(base, 256), lanes].astype(F32)
        x = jnp.where(rows_in < high, x, 0.0).astype(BF)
        spec = bdot(fwd_ref[...], x)
        xr, xi = spec[0:128], spec[128:256]
        hr, hi = spec_ref[0:128, lanes], spec_ref[128:256, lanes]
        prod = jnp.concatenate([xr * hr + xi * hi, xi * hr - xr * hi], 0).astype(BF)
        return bdot(inv_ref[0:count, :], prod)

    @pl.loop(0, 4)
    def _(b):
        base = pl.multiple_of(b * 128, 128)
        rows = pl.ds(base, 128)

        def one(t):
            stop = t + ahead_ref[t] + 1
            end = jnp.minimum(stop, base + 128)
            for half in range(2):
                lanes = pl.ds(half * 256, 256)
                out = correlate(base, stop - base, lanes, 128)
                keep = (rows_out >= t - base) & (rows_out < end - base)
                gu[:, lanes] = jnp.where(keep, out, gu[:, lanes])
            return end

        lax.while_loop(lambda t: t < base + 128, one, base)
        for g in range(4):
            lanes = pl.ds(g * 128, 128)
            part = gu[:, lanes]
            g_ext[4 + g, rows, :] = (part * vs_ref[rows, lanes].astype(F32)).astype(BF).astype(F32)
            g_ext[8 + g, rows, :] = (part * ks_ref[rows, lanes].astype(F32)).astype(BF).astype(F32)

    for half in range(2):
        lanes = pl.ds(half * 256, 256)
        part = correlate(512, ahead_ref[511], lanes, 16)
        gk = (part[0:8] * h[152:160, half * 256 : half * 256 + 256]).astype(BF).astype(F32)
        gv = (part[0:8] * h[144:152, half * 256 : half * 256 + 256]).astype(BF).astype(F32)
        for g in range(2):
            g_ext[4 + half * 2 + g, 512:520, :] = gk[:, g * 128 : g * 128 + 128]
            g_ext[8 + half * 2 + g, 512:520, :] = gv[:, g * 128 : g * 128 + 128]

    for c in range(8):
        start = c * 64

        def run(reach):
            for g in range(4):
                lanes = pl.ds(g * 128, 128)
                for s in range(3):
                    grad_ref[s, pl.ds(start, 64), lanes] = ahead_chunk(g_ext, s, start, w_ref, g, reach)

        both_ways(ahead_masked(back_ref, ahead_ref, start), row_ref, c // 2, c % 2, reach, run)


def backward(since, until, halo, gy, zed, qs, ks, vs, spec, short_filters, rows, fwd, inv):
    return pl.pallas_call(
        backward_kernel,
        in_specs=[sspec(), sspec()] + [vspec()] * 11,
        out_specs=vspec(),
        scratch_shapes=[
            VM((768, CH), BF),
            VM((12, TOK + 8, 128), F32),
            VM((128, CH), F32),
            VM((128, 128), F32),
        ],
        out_shape=jax.ShapeDtypeStruct((3, TOK, CH), BF),
        compiler_params=pltpu.CompilerParams(vmem_limit_bytes=LIMIT),
        name="backward_conv",
    )(since, until, halo, gy, zed, qs, ks, vs, spec, short_filters, rows, fwd, inv)


def body(proj, short_filters, long_filter, out_weight, cotangent, pack, since_start, until_end):
    fwd, inv_last, inv_first = dft_tables()
    back_rows = since_start.reshape(4, 128)
    ahead_rows = until_end.reshape(4, 128)
    msg = tail_message(since_start, until_end, proj, short_filters, back_rows)
    mixed, gy, halo_next, zed, qs, ks, vs, spec = products(
        pack, msg, out_weight, cotangent, proj, short_filters, long_filter, back_rows, ahead_rows,
        fwd, inv_last, *level_tables()
    )
    grad = backward(
        since_start, until_end, halo_next, gy, zed, qs, ks, vs, spec, short_filters, ahead_rows, fwd, inv_first
    )
    return (mixed, grad)


def solution(mesh):
    return jax.shard_map(
        body,
        mesh=mesh,
        in_specs=(
            P(None, "seq", "chan"),
            P(None, None, "chan"),
            P(None, "chan"),
            P("chan", "seq"),
            P("seq", "chan"),
            P(),
            P("seq"),
            P("seq"),
        ),
        out_specs=(P("seq", "chan"), P(None, "seq", "chan")),
        check_vma=False,
    )
```

```python
import functools

import jax
import jax.numpy as jnp
import numpy as np
from jax import lax
from jax.experimental import pallas as pl
from jax.experimental.pallas import tpu as pltpu
from jax.sharding import PartitionSpec as P

MESH = pl.DeviceIdType.MESH
BF = jnp.bfloat16
F32 = jnp.float32
TOK = 512
CH = 512
FILT = 128
SHORT = 7
MSG = 160
LIMIT = 56 << 20
VM = pltpu.VMEM


def vspec():
    return pl.BlockSpec(memory_space=pltpu.VMEM)


def sspec():
    return pl.BlockSpec(memory_space=pltpu.SMEM)


def dft_tables():
    k = np.arange(128)[:, None] + 0.5
    n = np.arange(256)[None, :]
    angle = 2 * np.pi * k * n / 256
    fwd = np.concatenate([np.cos(angle), -np.sin(angle)], 0)
    inv = np.concatenate([np.cos(angle), -np.sin(angle)], 0).T / 128
    return (
        jnp.asarray(fwd, BF),
        jnp.asarray(inv[128:], BF),
        jnp.asarray(inv[:128], BF),
    )


LEVELS = (64, 32, 16, 8)


def level_tables():
    fwd, inv, taps = [], [], []
    for run in LEVELS:
        pair = 2 * run
        k = np.arange(run)[:, None] + 0.5
        n = np.arange(pair)[None, :]
        angle = 2 * np.pi * k * n / pair
        cos, sin = np.cos(angle), np.sin(angle)
        first = (n < run).astype(np.float64)
        pairs = np.eye(256 // pair)
        fwd.append(np.concatenate([np.kron(pairs, cos * first), np.kron(pairs, -sin * first)], 0))
        last = 1.0 - first
        inv.append(
            np.concatenate([np.kron(pairs, cos * last), np.kron(pairs, -sin * last)], 0).T / run
        )
        wide = np.zeros((run, FILT))
        re, im = wide.copy(), wide.copy()
        re[:, :pair], im[:, :pair] = cos, -sin
        taps.append(np.concatenate([np.tile(re, (128 // run, 1)), np.tile(im, (128 // run, 1))], 0))
    return tuple(jnp.asarray(np.stack(t), BF) for t in (fwd, inv, taps))


def bdot(a, b):
    return jnp.dot(a, b, preferred_element_type=F32)


def reach_rows(row_ref, group):
    line = jnp.broadcast_to(row_ref[pl.ds(group, 1), :], (128, 128))
    return jnp.transpose(line.astype(F32))


def causal_chunk(ext, which, start, w_ref, g, reach):
    lanes = pl.ds(g * 128, 128)
    total = ext[which * 4 + g, pl.ds(start + 8, 64), :] * w_ref[which, 0:1, lanes]
    for i in range(1, SHORT):
        term = ext[which * 4 + g, pl.ds(start + 8 - i, 64), :] * w_ref[which, i : i + 1, lanes]
        if reach is not None:
            term = jnp.where(reach >= i, term, 0.0)
        total = total + term
    return total.astype(BF)


def ahead_chunk(ext, which, start, w_ref, g, reach):
    lanes = pl.ds(g * 128, 128)
    total = ext[which * 4 + g, pl.ds(start, 64), :] * w_ref[which, 0:1, lanes]
    for i in range(1, SHORT):
        term = ext[which * 4 + g, pl.ds(start + i, 64), :] * w_ref[which, i : i + 1, lanes]
        if reach is not None:
            term = jnp.where(reach >= i, term, 0.0)
        total = total + term
    return total.astype(BF)


def both_ways(is_masked, row_ref, group, half, reach, run):
    @pl.when(is_masked)
    def _():
        reach[...] = reach_rows(row_ref, group)
        run(reach[pl.ds(pl.multiple_of(half * 64, 64), 64), :])

    @pl.when(jnp.logical_not(is_masked))
    def _():
        run(None)


def ahead_masked(back_ref, ahead_ref, first):
    return (ahead_ref[first + 63] < SHORT - 1) | (back_ref[first + 63] < 63)


def place():
    s = lax.axis_index("seq")
    c = lax.axis_index("chan")
    return s // 2, s % 2, c // 4, c % 4


def dev(z, k, y, x):
    return (lax.rem(z + 8, 8) * 2 + k, lax.rem(y + 4, 4) * 4 + lax.rem(x + 4, 4))


def greet(targets):
    barrier = pltpu.get_barrier_semaphore()
    for t in targets:
        pl.semaphore_signal(barrier, inc=1, device_id=t, device_id_type=MESH)
    pl.semaphore_wait(barrier, len(targets))


def rcopy(src, dst, ssem, rsem, device):
    return pltpu.make_async_remote_copy(
        src_ref=src, dst_ref=dst, send_sem=ssem, recv_sem=rsem, device_id=device, device_id_type=MESH
    )


class SeqGather:
    def __init__(self, buf, r0, rows, send, recv):
        self.buf, self.r0, self.rows, self.send, self.recv = buf, r0, rows, send, recv
        self.z, self.k, self.y, self.x = place()
        self.sent = []
        self.from_sib = []
        self.seen = 0

    def view(self, z, k, part):
        s = lax.rem(z + 8, 8) * 2 + k
        half = self.rows // 2
        if part == 0:
            return self.buf.at[s, pl.ds(self.r0, self.rows)]
        return self.buf.at[s, pl.ds(self.r0 + (part - 1) * half, half)]

    def ring(self, way, hop):
        v = self.view(self.z - way * (hop - 1), self.k, 0 if hop < 4 else (1 if way > 0 else 2))
        n = (hop - 1) * 2 + (0 if way > 0 else 1)
        return rcopy(v, v, self.send.at[n], self.recv.at[n], dev(self.z + way, self.k, self.y, self.x))

    def landed(self, way, hop):
        v = self.view(self.z - way * hop, self.k, 0 if hop < 4 else (1 if way > 0 else 2))
        n = (hop - 1) * 2 + (0 if way > 0 else 1)
        rcopy(v, v, self.send.at[n], self.recv.at[n], dev(self.z + way, self.k, self.y, self.x)).wait_recv()

    def sib(self, offset, n):
        v = self.view(self.z + offset, self.k, 0)
        copy = rcopy(v, v, self.send.at[8 + n], self.recv.at[8 + n], dev(self.z, 1 - self.k, self.y, self.x))
        copy.start()
        self.sent.append(copy)
        w = self.view(self.z + offset, 1 - self.k, 0)
        self.from_sib.append(
            rcopy(w, w, self.send.at[8 + n], self.recv.at[8 + n], dev(self.z, 1 - self.k, self.y, self.x))
        )

    def go(self, way, hop):
        copy = self.ring(way, hop)
        copy.start()
        self.sent.append(copy)

    def begin(self):
        self.go(1, 1)
        self.go(-1, 1)
        self.sib(0, 0)

    def step(self, hop):
        for way in (1, -1):
            self.landed(way, hop)
            if hop < 4:
                self.go(way, hop + 1)
        if hop < 4:
            self.sib(-hop, 2 * hop - 1)
            self.sib(hop, 2 * hop)
        else:
            self.sib(4, 7)

    def arrived(self, count=8):
        while self.seen < count:
            self.from_sib[self.seen].wait_recv()
            self.seen += 1

    def finish(self):
        for copy in self.sent:
            copy.wait_send()


HALO_SUBS = ((0, 64), (64, 64), (128, 32))


def halo_gathers(buf, send, recv):
    return [SeqGather(buf, r0, rows, send.at[j], recv.at[j]) for j, (r0, rows) in enumerate(HALO_SUBS)]


def holder(pack_ref, seq, shift):
    wanted = pack_ref[seq] + shift
    found = jnp.int32(0)
    for i in range(16):
        found = found + jnp.where(pack_ref[i] == wanted, i, 0)
    return found


SUBS = 4
SUBROWS = 512 // SUBS
TILES = (pl.ds(0, 160), pl.ds(160, 352))


def product_kernel(
    pack_ref, w_ref, cot_own, proj_hbm, short_ref, long_ref, back_row, ahead_row,
    table_ref, inv_ref, lfwd_ref, linv_ref, ltaps_ref,
    mixed_ref, gy_ref, next_ref, z_ref, qs_ref, ks_ref, vs_ref, spec_ref,
    proj_ref, halo_ref, w_all, cot_all, y_all, gy_out, gy_in, mx_out, mx_in, ext, u_ext, back_b, ahead_b,
    local, swap, wsend, wrecv, asend, arecv, gsend, grecv, msend, mrecv, hsend, hrecv,
):
    z, k, y, x = place()
    s_own = z * 2 + k
    column = lax.rem(s_own, 4)
    target = dev(z + jnp.where(x == 2, 1, 0) - jnp.where(x == 3, 1, 0), lax.rem(x, 2), y, column)
    odd = lax.rem(z + x // 2, 2)
    source = dev(z + odd * (2 * k - 1), lax.rem(x, 2), y, k + 2 * odd)
    stays = (lax.rem(z, 2) == 0) & (k == x)

    def slot(o, a):
        plane = 2 * o + x // 2 + jnp.where(a == 2, 1, 0) - jnp.where(a == 3, 1, 0)
        return lax.rem(plane + 8, 8) * 2 + lax.rem(a, 2)

    mine = [
        pltpu.make_async_copy(cot_own, cot_all.at[y], local.at[1]),
    ]
    streams = pltpu.make_async_copy(proj_hbm, proj_ref, local.at[3])
    for copy in mine:
        copy.start()
    streams.start()
    barrier = pltpu.get_barrier_semaphore()
    for t in (
        dev(z + 1, k, y, x), dev(z - 1, k, y, x), dev(z, 1 - k, y, x),
        dev(z, k, y, x + 1), dev(z, k, y, x - 1), dev(z, k, y, x + 2),
        dev(z, k, y + 1, x), dev(z, k, y - 1, x), dev(z, k, y + 2, x),
    ):
        pl.semaphore_signal(barrier, inc=1, device_id=t, device_id_type=MESH)

    @pl.when(jnp.logical_not(stays))
    def _():
        for t in (target, source):
            pl.semaphore_signal(barrier, inc=1, device_id=t, device_id_type=MESH)


    sent = []

    def ring4(buf, me, at, base, r0, rows):
        def view(i, part):
            i = lax.rem(i + 4, 4)
            if part == 0:
                return buf.at[i, pl.ds(r0, rows)]
            return buf.at[i, pl.ds(r0 + (part - 1) * (rows // 2), rows // 2)]

        def copy(v, n, way):
            return rcopy(v, v, asend.at[base + n], arecv.at[base + n], at(way))

        def begin():
            for n, way in ((0, 1), (1, -1)):
                c = copy(view(me, 0), n, way)
                c.start()
                sent.append(c)

        def forward_on():
            for n, way in ((0, 1), (1, -1)):
                copy(view(me - way, 0), n, way).wait_recv()
                c = copy(view(me - way, 1 + n), 2 + n, way)
                c.start()
                sent.append(c)

        def end():
            for n, way in ((0, 1), (1, -1)):
                copy(view(me + 2, 1 + n), 2 + n, way).wait_recv()

        return begin, forward_on, end

    cot_begin, cot_on, cot_end = ring4(cot_all, y, lambda d: dev(z, k, y + d, x), 0, 0, 512)
    y_ring = [ring4(y_all, x, lambda d: dev(z, k, y, x + d), 4 + 4 * n, 256 * n, 256) for n in range(2)]

    subs = [SeqGather(w_all, j * SUBROWS, SUBROWS, wsend.at[j], wrecv.at[j]) for j in range(SUBS)]

    def gy_tile(p, a, m):
        rows = TILES[m]
        total = jnp.zeros((rows.size, 256), F32)
        for o in range(4):
            total = total + lax.dot_general(
                cot_all[o, rows, :], w_all[slot(o, a), pl.ds(p * 256, 256), :],
                (((1,), (1,)), ((), ())), preferred_element_type=F32,
            )
        gy_out[p, a, rows, :] = total.astype(BF)

    def gy_copy(p, a, m, rel):
        rows = TILES[m]
        n = (p * 2 + m) * 3 + rel - 1
        return rcopy(
            gy_out.at[p, a, rows], gy_in.at[p, rel - 1, rows], gsend.at[n], grecv.at[n], dev(z, k, y, a)
        )

    def mixed_part(o):
        @pl.loop(0, 4)
        def _(t):
            rows = pl.ds(pl.multiple_of((t // 2) * 256, 256), 256)
            cols = pl.ds(pl.multiple_of((t % 2) * 256, 256), 256)
            total = jnp.zeros((256, 256), F32)
            for a in range(4):
                total = total + bdot(y_all[a, rows, :], w_all[slot(o, a), :, cols])
            mx_out[o, rows, cols] = total.astype(BF)

    def gy_tiles(p, m):
        @pl.loop(0, 4)
        def _(i):
            rel = lax.rem(i + 1, 4)
            a = lax.rem(x + rel, 4)
            gy_tile(p, a, m)

    def gy_send(p, m):
        for rel in (2, 1, 3):
            c = gy_copy(p, lax.rem(x + rel, 4), m, rel)
            c.start()
            sent.append(c)

    def short_chunk(c):
        start = c * 64
        reach = back_b[start : start + 64, :]
        for g in range(4):
            lanes = pl.ds(g * 128, 128)
            got = [causal_chunk(ext, s, start, short_ref, g, reach) for s in range(3)]
            qs_ref[pl.ds(start, 64), lanes] = got[0]
            ks_ref[pl.ds(start, 64), lanes] = got[1]
            vs_ref[pl.ds(start, 64), lanes] = got[2]
            u_ext[g, pl.ds(start + 8, 64), :] = (got[1].astype(F32) * got[2].astype(F32)).astype(BF).astype(F32)

    def near_chunk(c):
        start = c * 64
        inside = lax.broadcasted_iota(jnp.int32, (64, 128), 0) % 8
        reach = jnp.minimum(back_b[start : start + 64, :], inside.astype(F32))
        for g in range(4):
            lanes = pl.ds(g * 128, 128)
            total = u_ext[g, pl.ds(start + 8, 64), :] * long_ref[0:1, lanes]
            for i in range(1, 8):
                term = u_ext[g, pl.ds(start + 8 - i, 64), :] * long_ref[i : i + 1, lanes]
                total = total + jnp.where(reach >= i, term, 0.0)
            z_ref[pl.ds(start, 64), lanes] = total

    def wide(mask):
        return jnp.concatenate([mask] * 2, axis=1)

    def times(spec, filt):
        n = spec.shape[0] // 2
        xr, xi, hr, hi = spec[:n], spec[n:], filt[:n], filt[n:]
        return jnp.concatenate([xr * hr - xi * hi, xr * hi + xi * hr], 0).astype(BF)

    def pairs_of_runs(batch):
        rows = pl.ds(batch * 256, 256)
        pos = lax.broadcasted_iota(jnp.int32, (256, 128), 0)

        @pl.loop(0, 4)
        def _(n):
            run = jnp.int32(64) >> n
            at = pos & (run - 1)
            second = (pos & run) != 0
            left = run - at
            into = jnp.where(
                jnp.logical_not(second) & (ahead_b[rows, :] >= left.astype(F32)), 1.0, 0.0
            )
            out = jnp.where(second & (back_b[rows, :] > at.astype(F32)), 1.0, 0.0)
            taps = bdot(ltaps_ref[n], long_ref[...].astype(BF))
            for half in range(2):
                lanes = pl.ds(half * 256, 256)
                u = jnp.concatenate(
                    [u_ext[half * 2 + g, pl.ds(batch * 256 + 8, 256), :] * into for g in range(2)], axis=1
                ).astype(BF)
                spec = bdot(lfwd_ref[n], u)
                prod = times(spec, taps[:, half * 256 : half * 256 + 256])
                z_ref[rows, lanes] += bdot(linv_ref[n], prod) * wide(out)

    def across(block, before):
        rows = pl.ds(block * 128, 128)
        pos = lax.broadcasted_iota(jnp.int32, (128, 128), 0)
        out = jnp.where(back_b[rows, :] > pos.astype(F32), 1.0, 0.0)
        for half in range(2):
            lanes = pl.ds(half * 256, 256)
            spec = bdot(table_ref[:, 0:128], before(half))
            prod = times(spec, spec_ref[:, lanes])
            z_ref[rows, lanes] += bdot(inv_ref[...], prod) * wide(out)

    def own_before(block):
        def get(half):
            pos = lax.broadcasted_iota(jnp.int32, (128, 128), 0)
            left = (128 - pos).astype(F32)
            into = jnp.where(ahead_b[pl.ds((block - 1) * 128, 128), :] >= left, 1.0, 0.0)
            return jnp.concatenate(
                [u_ext[half * 2 + g, pl.ds((block - 1) * 128 + 8, 128), :] * into for g in range(2)], axis=1
            ).astype(BF)

        return get

    def halo_before(half):
        pos = lax.broadcasted_iota(jnp.int32, (128, 128), 0)
        into = jnp.where(back_b[0:1, :] >= (128 - pos).astype(F32), 1.0, 0.0)
        return (got[0:128, half * 256 : half * 256 + 256].astype(F32) * wide(into)).astype(BF)

    def finish_y(batch):
        rows = pl.ds(batch * 256, 256)
        y_all[x, rows, :] = (qs_ref[rows, :].astype(F32) * z_ref[rows, :]).astype(BF)

    for g in range(4):
        back_b[g * 128 : g * 128 + 128, :] = reach_rows(back_row, g)
        ahead_b[g * 128 : g * 128 + 128, :] = reach_rows(ahead_row, g)
    streams.wait()
    for s in range(3):
        for g in range(4):
            ext[s * 4 + g, 8:520, :] = proj_ref[s, :, pl.ds(g * 128, 128)].astype(F32)
    for c in (7, 6):
        short_chunk(c)
    for g in range(4):
        lanes = pl.ds(g * 128, 128)
        halo_ref[0, s_own, 0:128, lanes] = u_ext[g, 392:520, :].astype(BF)
        halo_ref[0, s_own, 128:160, lanes] = jnp.concatenate(
            [ext[s * 4 + g, 512:520, :] for s in range(3)] + [jnp.zeros((8, 128), F32)], 0
        ).astype(BF)
    for copy in mine:
        copy.wait()

    @pl.when(jnp.logical_not(stays))
    def _():
        pl.semaphore_wait(barrier, 11)

    @pl.when(stays)
    def _():
        pl.semaphore_wait(barrier, 9)

    keep = pltpu.make_async_copy(w_ref, w_all.at[s_own], local.at[2])

    def swap_part(j, to):
        rows = pl.ds(j * SUBROWS, SUBROWS)
        return rcopy(w_ref.at[rows], w_all.at[to, rows], swap.at[0, j], swap.at[1, j], target)

    def swap_begin(parts):
        @pl.when(jnp.logical_not(stays))
        def _():
            for j in parts:
                swap_part(j, target[0]).start()

    @pl.when(stays)
    def _():
        keep.start()
        keep.wait()

    swap_begin((0, 1))
    early = halo_gathers(halo_ref.at[0], hsend.at[0], hrecv.at[0])
    for g in early:
        g.begin()
    def swapped(j):
        @pl.when(jnp.logical_not(stays))
        def _():
            swap_part(j, s_own).wait_recv()
            swap_part(j, target[0]).wait_send()

    def gy_phase(p, m):
        gy_tiles(p, m)
        gy_send(p, m)

    cot_begin()
    def hop(group, n):
        for g in group:
            g.step(n)

    first, second = subs[:2], subs[2:]
    for c in (5, 4):
        short_chunk(c)
    hop(early, 1)
    spec_ref[...] = bdot(table_ref[:, 0:128], long_ref[...].astype(BF))
    hop(early, 2)
    for j in range(2):
        swapped(j)
        subs[j].begin()
    swap_begin((2, 3))
    for c in (3, 2, 1):
        short_chunk(c)
    hop(early, 3)
    cot_on()
    for c in range(4, 8):
        near_chunk(c)
    pairs_of_runs(1)
    hop(early, 4)
    hop(first, 1)
    across(2, own_before(2))
    across(3, own_before(3))
    finish_y(1)
    y_ring[1][0]()
    for g in early:
        g.arrived()
    got = halo_ref[0, holder(pack_ref, s_own, -1)]
    raw = got[128:160, :].astype(F32)
    for s in range(3):
        for g in range(4):
            ext[s * 4 + g, 0:8, :] = raw[s * 8 : s * 8 + 8, g * 128 : g * 128 + 128]
    short_chunk(0)
    hop(first, 2)
    swapped(2)
    subs[2].begin()
    for c in range(4):
        near_chunk(c)
    pairs_of_runs(0)
    across(0, halo_before)
    across(1, own_before(1))
    finish_y(0)
    y_ring[0][0]()
    hop(first, 3)
    swapped(3)
    subs[3].begin()
    y_ring[1][1]()
    hop(first, 4)
    for g in first:
        g.arrived()
    cot_end()
    gy_phase(0, 0)
    y_ring[0][1]()
    hop(second, 1)
    gy_phase(0, 1)
    y_ring[1][2]()
    y_ring[0][2]()

    def mixed_copy(rel):
        o = lax.rem(y + rel, 4)
        slot = jnp.maximum(rel - 1, 0)
        return rcopy(mx_out.at[o], mx_in.at[slot], msend.at[slot], mrecv.at[slot], dev(z, k, o, x))

    def mixed_send(o):
        mixed_part(o)
        rel = lax.rem(o - y + 4, 4)

        @pl.when(rel != 0)
        def _():
            mixed_copy(rel).start()

    centre = (z + odd - x // 2 + 8) // 2

    def nth(n):
        return lax.rem(centre + jnp.where(odd == 1, (0, 3, 1, 2)[n], (0, 1, 3, 2)[n]), 4)

    hop(second, 2)
    for g in second:
        g.arrived(5)
    mixed_send(nth(0))
    hop(second, 3)
    for g in second:
        g.arrived(7)
    mixed_send(nth(1))
    hop(second, 4)
    for g in second:
        g.arrived()
    gy_phase(1, 0)
    mixed_send(nth(2))
    gy_tiles(1, 1)
    mixed_send(nth(3))

    def gy_sum(m):
        rows = TILES[m]
        for p in range(2):
            for rel in (1, 2, 3):
                gy_copy(p, lax.rem(x + rel, 4), m, rel).wait_recv()
            total = gy_out[p, x, rows, :].astype(F32)
            for r in range(3):
                total = total + gy_in[p, r, rows, :].astype(F32)
            gy_ref[rows, p * 256 : p * 256 + 256] = total.astype(BF)

    gy_sum(0)
    head = gy_ref[0:144, :].astype(F32)
    gz = head[0:136] * qs_ref[0:144, :].astype(F32)[0:136]
    gq = head[0:8] * z_ref[0:8, :]
    halo_ref[1, s_own] = jnp.concatenate(
        [gz, gq, ks_ref[0:16, :].astype(F32)[0:8], vs_ref[0:16, :].astype(F32)[0:8]], 0
    ).astype(BF)
    parts = halo_gathers(halo_ref.at[1], hsend.at[1], hrecv.at[1])
    for g in parts:
        g.begin()
    gy_send(1, 1)
    for n in (1, 2, 3):
        hop(parts, n)
    gy_sum(1)
    hop(parts, 4)

    for rel in (1, 2, 3):
        mixed_copy(jnp.int32(rel)).wait_recv()
        mixed_copy(jnp.int32(rel)).wait_send()

    @pl.loop(0, 4)
    def _(t):
        rows = pl.ds(pl.multiple_of(t * 128, 128), 128)
        total = mx_out[y, rows, :].astype(F32)
        for r in range(3):
            total = total + mx_in[r, rows, :].astype(F32)
        mixed_ref[rows, :] = total.astype(BF)

    for g in parts:
        g.arrived()
    next_ref[...] = halo_ref[1, holder(pack_ref, s_own, 1)]
    for g in parts:
        g.finish()
    for g in early + subs:
        g.finish()
    for c in sent:
        c.wait_send()


def products(*args):
    out = jax.ShapeDtypeStruct((TOK, CH), BF)
    dma = pltpu.SemaphoreType.DMA
    return pl.pallas_call(
        product_kernel,
        out_shape=[
            out,
            out,
            jax.ShapeDtypeStruct((MSG, CH), BF),
            jax.ShapeDtypeStruct((TOK, CH), F32),
            out,
            out,
            out,
            jax.ShapeDtypeStruct((256, CH), F32),
        ],
        in_specs=[sspec()] + [pl.BlockSpec(memory_space=pl.ANY)] * 3 + [vspec()] * 9,
        out_specs=[vspec()] * 8,
        scratch_shapes=[
            VM((3, TOK, CH), BF),
            VM((2, 16, MSG, CH), BF),
            VM((16, 512, 512), BF),
            VM((4, 512, 512), BF),
            VM((4, 512, 512), BF),
            VM((2, 4, 512, 256), BF),
            VM((2, 3, 512, 256), BF),
            VM((4, 512, 512), BF),
            VM((3, 512, 512), BF),
            VM((12, TOK + 8, 128), F32),
            VM((4, TOK + 8, 128), F32),
            VM((TOK, 128), F32),
            VM((TOK, 128), F32),
            dma((4,)),
            dma((2, SUBS)),
            dma((SUBS, 16)),
            dma((SUBS, 16)),
            dma((12,)),
            dma((12,)),
            dma((12,)),
            dma((12,)),
            dma((3,)),
            dma((3,)),
            dma((2, 3, 16)),
            dma((2, 3, 16)),
        ],
        compiler_params=pltpu.CompilerParams(
            collective_id=2, has_side_effects=True, vmem_limit_bytes=LIMIT
        ),
        name="products",
    )(*args)


def backward_kernel(
    back_ref, ahead_ref, halo_ref, gy_ref, z_ref, qs_ref, ks_ref, vs_ref, spec_ref, w_ref, row_ref,
    fwd_ref, inv_ref,
    grad_ref, gz_ext, g_ext, gu, reach,
):
    h = halo_ref[...].astype(F32)
    gz_ext[512:656, :] = h[0:144, :].astype(BF)
    gz_ext[656:768, :] = jnp.zeros((112, CH), BF)
    for g in range(4):
        g_ext[g, 512:520, :] = h[136:144, g * 128 : g * 128 + 128]

    @pl.loop(0, 8)
    def _(c):
        rows = pl.ds(pl.multiple_of(c * 64, 64), 64)
        gy = gy_ref[rows, :].astype(F32)
        gz_ext[rows, :] = (gy * qs_ref[rows, :].astype(F32)).astype(BF)
        gq = (gy * z_ref[rows, :]).astype(BF).astype(F32)
        for g in range(4):
            g_ext[g, rows, :] = gq[:, g * 128 : g * 128 + 128]

    rows_in = lax.broadcasted_iota(jnp.int32, (256, 256), 0)
    rows_out = lax.broadcasted_iota(jnp.int32, (128, 256), 0)

    def correlate(base, high, lanes, count):
        x = gz_ext[pl.ds(base, 256), lanes].astype(F32)
        x = jnp.where(rows_in < high, x, 0.0).astype(BF)
        spec = bdot(fwd_ref[...], x)
        xr, xi = spec[0:128], spec[128:256]
        hr, hi = spec_ref[0:128, lanes], spec_ref[128:256, lanes]
        prod = jnp.concatenate([xr * hr + xi * hi, xi * hr - xr * hi], 0).astype(BF)
        return bdot(inv_ref[0:count, :], prod)

    @pl.loop(0, 4)
    def _(b):
        base = pl.multiple_of(b * 128, 128)
        rows = pl.ds(base, 128)

        def one(t):
            stop = t + ahead_ref[t] + 1
            end = jnp.minimum(stop, base + 128)
            for half in range(2):
                lanes = pl.ds(half * 256, 256)
                out = correlate(base, stop - base, lanes, 128)
                keep = (rows_out >= t - base) & (rows_out < end - base)
                gu[:, lanes] = jnp.where(keep, out, gu[:, lanes])
            return end

        lax.while_loop(lambda t: t < base + 128, one, base)
        for g in range(4):
            lanes = pl.ds(g * 128, 128)
            part = gu[:, lanes]
            g_ext[4 + g, rows, :] = (part * vs_ref[rows, lanes].astype(F32)).astype(BF).astype(F32)
            g_ext[8 + g, rows, :] = (part * ks_ref[rows, lanes].astype(F32)).astype(BF).astype(F32)

    for half in range(2):
        lanes = pl.ds(half * 256, 256)
        part = correlate(512, ahead_ref[511], lanes, 16)
        gk = (part[0:8] * h[152:160, half * 256 : half * 256 + 256]).astype(BF).astype(F32)
        gv = (part[0:8] * h[144:152, half * 256 : half * 256 + 256]).astype(BF).astype(F32)
        for g in range(2):
            g_ext[4 + half * 2 + g, 512:520, :] = gk[:, g * 128 : g * 128 + 128]
            g_ext[8 + half * 2 + g, 512:520, :] = gv[:, g * 128 : g * 128 + 128]

    for c in range(8):
        start = c * 64

        def run(reach):
            for g in range(4):
                lanes = pl.ds(g * 128, 128)
                for s in range(3):
                    grad_ref[s, pl.ds(start, 64), lanes] = ahead_chunk(g_ext, s, start, w_ref, g, reach)

        both_ways(ahead_masked(back_ref, ahead_ref, start), row_ref, c // 2, c % 2, reach, run)


def backward(since, until, halo, gy, zed, qs, ks, vs, spec, short_filters, rows, fwd, inv):
    return pl.pallas_call(
        backward_kernel,
        in_specs=[sspec(), sspec()] + [vspec()] * 11,
        out_specs=vspec(),
        scratch_shapes=[
            VM((768, CH), BF),
            VM((12, TOK + 8, 128), F32),
            VM((128, CH), F32),
            VM((128, 128), F32),
        ],
        out_shape=jax.ShapeDtypeStruct((3, TOK, CH), BF),
        compiler_params=pltpu.CompilerParams(vmem_limit_bytes=LIMIT),
        name="backward_conv",
    )(since, until, halo, gy, zed, qs, ks, vs, spec, short_filters, rows, fwd, inv)


def body(proj, short_filters, long_filter, out_weight, cotangent, pack, since_start, until_end):
    fwd, inv_last, inv_first = dft_tables()
    back_rows = since_start.reshape(4, 128)
    ahead_rows = until_end.reshape(4, 128)
    mixed, gy, halo_next, zed, qs, ks, vs, spec = products(
        pack, out_weight, cotangent, proj, short_filters, long_filter, back_rows, ahead_rows,
        fwd, inv_last, *level_tables()
    )
    grad = backward(
        since_start, until_end, halo_next, gy, zed, qs, ks, vs, spec, short_filters, ahead_rows, fwd, inv_first
    )
    return (mixed, grad)


def solution(mesh):
    return jax.shard_map(
        body,
        mesh=mesh,
        in_specs=(
            P(None, "seq", "chan"),
            P(None, None, "chan"),
            P(None, "chan"),
            P("chan", "seq"),
            P("seq", "chan"),
            P(),
            P("seq"),
            P("seq"),
        ),
        out_specs=(P("seq", "chan"), P(None, "seq", "chan")),
        check_vma=False,
    )
```

```python
import functools

import jax
import jax.numpy as jnp
import numpy as np
from jax import lax
from jax.experimental import pallas as pl
from jax.experimental.pallas import tpu as pltpu
from jax.sharding import PartitionSpec as P

MESH = pl.DeviceIdType.MESH
BF = jnp.bfloat16
F32 = jnp.float32
TOK = 512
CH = 512
FILT = 128
SHORT = 7
MSG = 160
LIMIT = 56 << 20
VM = pltpu.VMEM


def vspec():
    return pl.BlockSpec(memory_space=pltpu.VMEM)


def sspec():
    return pl.BlockSpec(memory_space=pltpu.SMEM)


def dft_tables():
    k = np.arange(128)[:, None] + 0.5
    n = np.arange(256)[None, :]
    angle = 2 * np.pi * k * n / 256
    fwd = np.concatenate([np.cos(angle), -np.sin(angle)], 0)
    inv = np.concatenate([np.cos(angle), -np.sin(angle)], 0).T / 128
    return (
        jnp.asarray(fwd, BF),
        jnp.asarray(inv[128:], BF),
        jnp.asarray(inv[:128], BF),
    )


LEVELS = (64, 32, 16, 8)


def level_tables():
    fwd, inv, taps = [], [], []
    for run in LEVELS:
        pair = 2 * run
        k = np.arange(run)[:, None] + 0.5
        n = np.arange(pair)[None, :]
        angle = 2 * np.pi * k * n / pair
        cos, sin = np.cos(angle), np.sin(angle)
        first = (n < run).astype(np.float64)
        pairs = np.eye(256 // pair)
        fwd.append(np.concatenate([np.kron(pairs, cos * first), np.kron(pairs, -sin * first)], 0))
        last = 1.0 - first
        inv.append(
            np.concatenate([np.kron(pairs, cos * last), np.kron(pairs, -sin * last)], 0).T / run
        )
        wide = np.zeros((run, FILT))
        re, im = wide.copy(), wide.copy()
        re[:, :pair], im[:, :pair] = cos, -sin
        taps.append(np.concatenate([np.tile(re, (128 // run, 1)), np.tile(im, (128 // run, 1))], 0))
    return tuple(jnp.asarray(np.stack(t), BF) for t in (fwd, inv, taps))


def bdot(a, b):
    return jnp.dot(a, b, preferred_element_type=F32)


def reach_rows(row_ref, group):
    line = jnp.broadcast_to(row_ref[pl.ds(group, 1), :], (128, 128))
    return jnp.transpose(line.astype(F32))


def causal_chunk(ext, which, start, w_ref, g, reach):
    lanes = pl.ds(g * 128, 128)
    total = ext[which * 4 + g, pl.ds(start + 8, 64), :] * w_ref[which, 0:1, lanes]
    for i in range(1, SHORT):
        term = ext[which * 4 + g, pl.ds(start + 8 - i, 64), :] * w_ref[which, i : i + 1, lanes]
        if reach is not None:
            term = jnp.where(reach >= i, term, 0.0)
        total = total + term
    return total.astype(BF)


def ahead_chunk(ext, which, start, w_ref, g, reach):
    lanes = pl.ds(g * 128, 128)
    total = ext[which * 4 + g, pl.ds(start, 64), :] * w_ref[which, 0:1, lanes]
    for i in range(1, SHORT):
        term = ext[which * 4 + g, pl.ds(start + i, 64), :] * w_ref[which, i : i + 1, lanes]
        if reach is not None:
            term = jnp.where(reach >= i, term, 0.0)
        total = total + term
    return total.astype(BF)


def both_ways(is_masked, row_ref, group, half, reach, run):
    @pl.when(is_masked)
    def _():
        reach[...] = reach_rows(row_ref, group)
        run(reach[pl.ds(pl.multiple_of(half * 64, 64), 64), :])

    @pl.when(jnp.logical_not(is_masked))
    def _():
        run(None)


def ahead_masked(back_ref, ahead_ref, first):
    return (ahead_ref[first + 63] < SHORT - 1) | (back_ref[first + 63] < 63)


def place():
    s = lax.axis_index("seq")
    c = lax.axis_index("chan")
    return s // 2, s % 2, c // 4, c % 4


def dev(z, k, y, x):
    return (lax.rem(z + 8, 8) * 2 + k, lax.rem(y + 4, 4) * 4 + lax.rem(x + 4, 4))


def greet(targets):
    barrier = pltpu.get_barrier_semaphore()
    for t in targets:
        pl.semaphore_signal(barrier, inc=1, device_id=t, device_id_type=MESH)
    pl.semaphore_wait(barrier, len(targets))


def rcopy(src, dst, ssem, rsem, device):
    return pltpu.make_async_remote_copy(
        src_ref=src, dst_ref=dst, send_sem=ssem, recv_sem=rsem, device_id=device, device_id_type=MESH
    )


class SeqGather:
    def __init__(self, buf, r0, rows, send, recv):
        self.buf, self.r0, self.rows, self.send, self.recv = buf, r0, rows, send, recv
        self.z, self.k, self.y, self.x = place()
        self.sent = []
        self.from_sib = []
        self.seen = 0

    def view(self, z, k, part):
        s = lax.rem(z + 8, 8) * 2 + k
        half = self.rows // 2
        if part == 0:
            return self.buf.at[s, pl.ds(self.r0, self.rows)]
        return self.buf.at[s, pl.ds(self.r0 + (part - 1) * half, half)]

    def ring(self, way, hop):
        v = self.view(self.z - way * (hop - 1), self.k, 0 if hop < 4 else (1 if way > 0 else 2))
        n = (hop - 1) * 2 + (0 if way > 0 else 1)
        return rcopy(v, v, self.send.at[n], self.recv.at[n], dev(self.z + way, self.k, self.y, self.x))

    def landed(self, way, hop):
        v = self.view(self.z - way * hop, self.k, 0 if hop < 4 else (1 if way > 0 else 2))
        n = (hop - 1) * 2 + (0 if way > 0 else 1)
        rcopy(v, v, self.send.at[n], self.recv.at[n], dev(self.z + way, self.k, self.y, self.x)).wait_recv()

    def sib(self, offset, n):
        v = self.view(self.z + offset, self.k, 0)
        copy = rcopy(v, v, self.send.at[8 + n], self.recv.at[8 + n], dev(self.z, 1 - self.k, self.y, self.x))
        copy.start()
        self.sent.append(copy)
        w = self.view(self.z + offset, 1 - self.k, 0)
        self.from_sib.append(
            rcopy(w, w, self.send.at[8 + n], self.recv.at[8 + n], dev(self.z, 1 - self.k, self.y, self.x))
        )

    def go(self, way, hop):
        copy = self.ring(way, hop)
        copy.start()
        self.sent.append(copy)

    def begin(self):
        self.go(1, 1)
        self.go(-1, 1)
        self.sib(0, 0)

    def step(self, hop):
        for way in (1, -1):
            self.landed(way, hop)
            if hop < 4:
                self.go(way, hop + 1)
        if hop < 4:
            self.sib(-hop, 2 * hop - 1)
            self.sib(hop, 2 * hop)
        else:
            self.sib(4, 7)

    def arrived(self, count=8):
        while self.seen < count:
            self.from_sib[self.seen].wait_recv()
            self.seen += 1

    def finish(self):
        for copy in self.sent:
            copy.wait_send()


HALO_SUBS = ((0, 64), (64, 64), (128, 32))


def halo_gathers(buf, send, recv):
    return [SeqGather(buf, r0, rows, send.at[j], recv.at[j]) for j, (r0, rows) in enumerate(HALO_SUBS)]


def holder(pack_ref, seq, shift):
    wanted = pack_ref[seq] + shift
    found = jnp.int32(0)
    for i in range(16):
        found = found + jnp.where(pack_ref[i] == wanted, i, 0)
    return found


SUBS = 4
SUBROWS = 512 // SUBS
TILES = (pl.ds(0, 160), pl.ds(160, 352))


def product_kernel(
    pack_ref, w_ref, cot_own, proj_hbm, short_ref, long_ref, back_row, ahead_row,
    table_ref, inv_ref, lfwd_hbm, linv_hbm, ltaps_hbm,
    mixed_ref, gy_ref, next_ref, z_hbm, qs_hbm, ks_hbm, vs_hbm, spec_hbm,
    lfwd_ref, linv_ref, ltaps_ref, z_ref, qs_ref, ks_ref, vs_ref, spec_ref, proj_ref, halo_ref, w_all, cot_all, y_all, gy_out, gy_in, mx_out, mx_in, ext, u_ext, back_b, ahead_b,
    local, swap, wsend, wrecv, asend, arecv, gsend, grecv, msend, mrecv, hsend, hrecv,
):
    z, k, y, x = place()
    s_own = z * 2 + k
    column = lax.rem(s_own, 4)
    target = dev(z + jnp.where(x == 2, 1, 0) - jnp.where(x == 3, 1, 0), lax.rem(x, 2), y, column)
    odd = lax.rem(z + x // 2, 2)
    source = dev(z + odd * (2 * k - 1), lax.rem(x, 2), y, k + 2 * odd)
    stays = (lax.rem(z, 2) == 0) & (k == x)

    def slot(o, a):
        plane = 2 * o + x // 2 + jnp.where(a == 2, 1, 0) - jnp.where(a == 3, 1, 0)
        return lax.rem(plane + 8, 8) * 2 + lax.rem(a, 2)

    mine = [
        pltpu.make_async_copy(cot_own, cot_all.at[y], local.at[1]),
    ]
    streams = pltpu.make_async_copy(proj_hbm, proj_ref, local.at[3])
    for copy in mine:
        copy.start()
    streams.start()
    tables = [
        pltpu.make_async_copy(lfwd_hbm, lfwd_ref, local.at[4]),
        pltpu.make_async_copy(linv_hbm, linv_ref, local.at[5]),
        pltpu.make_async_copy(ltaps_hbm, ltaps_ref, local.at[6]),
    ]
    results = [
        pltpu.make_async_copy(z_ref, z_hbm, local.at[7]),
        pltpu.make_async_copy(qs_ref, qs_hbm, local.at[8]),
        pltpu.make_async_copy(ks_ref, ks_hbm, local.at[9]),
        pltpu.make_async_copy(vs_ref, vs_hbm, local.at[10]),
        pltpu.make_async_copy(spec_ref, spec_hbm, local.at[11]),
    ]
    for copy in tables:
        copy.start()
    barrier = pltpu.get_barrier_semaphore()
    for t in (
        dev(z + 1, k, y, x), dev(z - 1, k, y, x), dev(z, 1 - k, y, x),
        dev(z, k, y, x + 1), dev(z, k, y, x - 1), dev(z, k, y, x + 2),
        dev(z, k, y + 1, x), dev(z, k, y - 1, x), dev(z, k, y + 2, x),
    ):
        pl.semaphore_signal(barrier, inc=1, device_id=t, device_id_type=MESH)

    @pl.when(jnp.logical_not(stays))
    def _():
        for t in (target, source):
            pl.semaphore_signal(barrier, inc=1, device_id=t, device_id_type=MESH)


    sent = []

    def ring4(buf, me, at, base, r0, rows):
        def view(i, part):
            i = lax.rem(i + 4, 4)
            if part == 0:
                return buf.at[i, pl.ds(r0, rows)]
            return buf.at[i, pl.ds(r0 + (part - 1) * (rows // 2), rows // 2)]

        def copy(v, n, way):
            return rcopy(v, v, asend.at[base + n], arecv.at[base + n], at(way))

        def begin():
            for n, way in ((0, 1), (1, -1)):
                c = copy(view(me, 0), n, way)
                c.start()
                sent.append(c)

        def forward_on():
            for n, way in ((0, 1), (1, -1)):
                copy(view(me - way, 0), n, way).wait_recv()
                c = copy(view(me - way, 1 + n), 2 + n, way)
                c.start()
                sent.append(c)

        def end():
            for n, way in ((0, 1), (1, -1)):
                copy(view(me + 2, 1 + n), 2 + n, way).wait_recv()

        return begin, forward_on, end

    cot_begin, cot_on, cot_end = ring4(cot_all, y, lambda d: dev(z, k, y + d, x), 0, 0, 512)
    y_ring = [ring4(y_all, x, lambda d: dev(z, k, y, x + d), 4 + 4 * n, 256 * n, 256) for n in range(2)]

    subs = [SeqGather(w_all, j * SUBROWS, SUBROWS, wsend.at[j], wrecv.at[j]) for j in range(SUBS)]

    def gy_tile(p, a, m):
        rows = TILES[m]
        total = jnp.zeros((rows.size, 256), F32)
        for o in range(4):
            total = total + lax.dot_general(
                cot_all[o, rows, :], w_all[slot(o, a), pl.ds(p * 256, 256), :],
                (((1,), (1,)), ((), ())), preferred_element_type=F32,
            )
        gy_out[p, a, rows, :] = total.astype(BF)

    def gy_copy(p, a, m, rel):
        rows = TILES[m]
        n = (p * 2 + m) * 3 + rel - 1
        return rcopy(
            gy_out.at[p, a, rows], gy_in.at[p, rel - 1, rows], gsend.at[n], grecv.at[n], dev(z, k, y, a)
        )

    def mixed_part(o):
        @pl.loop(0, 4)
        def _(t):
            rows = pl.ds(pl.multiple_of((t // 2) * 256, 256), 256)
            cols = pl.ds(pl.multiple_of((t % 2) * 256, 256), 256)
            total = jnp.zeros((256, 256), F32)
            for a in range(4):
                total = total + bdot(y_all[a, rows, :], w_all[slot(o, a), :, cols])
            mx_out[o, rows, cols] = total.astype(BF)

    def gy_tiles(p, m):
        @pl.loop(0, 4)
        def _(i):
            rel = lax.rem(i + 1, 4)
            a = lax.rem(x + rel, 4)
            gy_tile(p, a, m)

    def gy_send(p, m):
        for rel in (2, 1, 3):
            c = gy_copy(p, lax.rem(x + rel, 4), m, rel)
            c.start()
            sent.append(c)

    def short_chunk(c):
        start = c * 64
        reach = back_b[start : start + 64, :]
        for g in range(4):
            lanes = pl.ds(g * 128, 128)
            got = [causal_chunk(ext, s, start, short_ref, g, reach) for s in range(3)]
            qs_ref[pl.ds(start, 64), lanes] = got[0]
            ks_ref[pl.ds(start, 64), lanes] = got[1]
            vs_ref[pl.ds(start, 64), lanes] = got[2]
            u_ext[g, pl.ds(start + 8, 64), :] = (got[1].astype(F32) * got[2].astype(F32)).astype(BF).astype(F32)

    def near_chunk(c):
        start = c * 64
        inside = lax.broadcasted_iota(jnp.int32, (64, 128), 0) % 8
        reach = jnp.minimum(back_b[start : start + 64, :], inside.astype(F32))
        for g in range(4):
            lanes = pl.ds(g * 128, 128)
            total = u_ext[g, pl.ds(start + 8, 64), :] * long_ref[0:1, lanes]
            for i in range(1, 8):
                term = u_ext[g, pl.ds(start + 8 - i, 64), :] * long_ref[i : i + 1, lanes]
                total = total + jnp.where(reach >= i, term, 0.0)
            z_ref[pl.ds(start, 64), lanes] = total

    def wide(mask):
        return jnp.concatenate([mask] * 2, axis=1)

    def times(spec, filt):
        n = spec.shape[0] // 2
        xr, xi, hr, hi = spec[:n], spec[n:], filt[:n], filt[n:]
        return jnp.concatenate([xr * hr - xi * hi, xr * hi + xi * hr], 0).astype(BF)

    def pairs_of_runs(batch):
        rows = pl.ds(batch * 256, 256)
        pos = lax.broadcasted_iota(jnp.int32, (256, 128), 0)

        @pl.loop(0, 4)
        def _(n):
            run = jnp.int32(64) >> n
            at = pos & (run - 1)
            second = (pos & run) != 0
            left = run - at
            into = jnp.where(
                jnp.logical_not(second) & (ahead_b[rows, :] >= left.astype(F32)), 1.0, 0.0
            )
            out = jnp.where(second & (back_b[rows, :] > at.astype(F32)), 1.0, 0.0)
            taps = bdot(ltaps_ref[n], long_ref[...].astype(BF))
            for half in range(2):
                lanes = pl.ds(half * 256, 256)
                u = jnp.concatenate(
                    [u_ext[half * 2 + g, pl.ds(batch * 256 + 8, 256), :] * into for g in range(2)], axis=1
                ).astype(BF)
                spec = bdot(lfwd_ref[n], u)
                prod = times(spec, taps[:, half * 256 : half * 256 + 256])
                z_ref[rows, lanes] += bdot(linv_ref[n], prod) * wide(out)

    def across(block, before):
        rows = pl.ds(block * 128, 128)
        pos = lax.broadcasted_iota(jnp.int32, (128, 128), 0)
        out = jnp.where(back_b[rows, :] > pos.astype(F32), 1.0, 0.0)
        for half in range(2):
            lanes = pl.ds(half * 256, 256)
            spec = bdot(table_ref[:, 0:128], before(half))
            prod = times(spec, spec_ref[:, lanes])
            z_ref[rows, lanes] += bdot(inv_ref[...], prod) * wide(out)

    def own_before(block):
        def get(half):
            pos = lax.broadcasted_iota(jnp.int32, (128, 128), 0)
            left = (128 - pos).astype(F32)
            into = jnp.where(ahead_b[pl.ds((block - 1) * 128, 128), :] >= left, 1.0, 0.0)
            return jnp.concatenate(
                [u_ext[half * 2 + g, pl.ds((block - 1) * 128 + 8, 128), :] * into for g in range(2)], axis=1
            ).astype(BF)

        return get

    def halo_before(half):
        pos = lax.broadcasted_iota(jnp.int32, (128, 128), 0)
        into = jnp.where(back_b[0:1, :] >= (128 - pos).astype(F32), 1.0, 0.0)
        return (got[0:128, half * 256 : half * 256 + 256].astype(F32) * wide(into)).astype(BF)

    def finish_y(batch):
        rows = pl.ds(batch * 256, 256)
        y_all[x, rows, :] = (qs_ref[rows, :].astype(F32) * z_ref[rows, :]).astype(BF)

    for g in range(4):
        back_b[g * 128 : g * 128 + 128, :] = reach_rows(back_row, g)
        ahead_b[g * 128 : g * 128 + 128, :] = reach_rows(ahead_row, g)
    streams.wait()
    for s in range(3):
        for g in range(4):
            ext[s * 4 + g, 8:520, :] = proj_ref[s, :, pl.ds(g * 128, 128)].astype(F32)
    for c in (7, 6):
        short_chunk(c)
    for g in range(4):
        lanes = pl.ds(g * 128, 128)
        halo_ref[0, s_own, 0:128, lanes] = u_ext[g, 392:520, :].astype(BF)
        halo_ref[0, s_own, 128:160, lanes] = jnp.concatenate(
            [ext[s * 4 + g, 512:520, :] for s in range(3)] + [jnp.zeros((8, 128), F32)], 0
        ).astype(BF)
    for copy in mine:
        copy.wait()

    @pl.when(jnp.logical_not(stays))
    def _():
        pl.semaphore_wait(barrier, 11)

    @pl.when(stays)
    def _():
        pl.semaphore_wait(barrier, 9)

    keep = pltpu.make_async_copy(w_ref, w_all.at[s_own], local.at[2])

    def swap_part(j, to):
        rows = pl.ds(j * SUBROWS, SUBROWS)
        return rcopy(w_ref.at[rows], w_all.at[to, rows], swap.at[0, j], swap.at[1, j], target)

    def swap_begin(parts):
        @pl.when(jnp.logical_not(stays))
        def _():
            for j in parts:
                swap_part(j, target[0]).start()

    @pl.when(stays)
    def _():
        keep.start()
        keep.wait()

    swap_begin((0, 1))
    early = halo_gathers(halo_ref.at[0], hsend.at[0], hrecv.at[0])
    for g in early:
        g.begin()
    def swapped(j):
        @pl.when(jnp.logical_not(stays))
        def _():
            swap_part(j, s_own).wait_recv()
            swap_part(j, target[0]).wait_send()

    def gy_phase(p, m):
        gy_tiles(p, m)
        gy_send(p, m)

    cot_begin()
    def hop(group, n):
        for g in group:
            g.step(n)

    first, second = subs[:2], subs[2:]
    for c in (5, 4):
        short_chunk(c)
    hop(early, 1)
    spec_ref[...] = bdot(table_ref[:, 0:128], long_ref[...].astype(BF))
    hop(early, 2)
    for j in range(2):
        swapped(j)
        subs[j].begin()
    swap_begin((2, 3))
    for c in (3, 2, 1):
        short_chunk(c)
    hop(early, 3)
    cot_on()
    for c in range(4, 8):
        near_chunk(c)
    for copy in tables:
        copy.wait()
    pairs_of_runs(1)
    hop(early, 4)
    hop(first, 1)
    across(2, own_before(2))
    across(3, own_before(3))
    finish_y(1)
    y_ring[1][0]()
    for g in early:
        g.arrived()
    got = halo_ref[0, holder(pack_ref, s_own, -1)]
    raw = got[128:160, :].astype(F32)
    for s in range(3):
        for g in range(4):
            ext[s * 4 + g, 0:8, :] = raw[s * 8 : s * 8 + 8, g * 128 : g * 128 + 128]
    short_chunk(0)
    hop(first, 2)
    swapped(2)
    subs[2].begin()
    for c in range(4):
        near_chunk(c)
    pairs_of_runs(0)
    across(0, halo_before)
    across(1, own_before(1))
    finish_y(0)
    for copy in results:
        copy.start()
    y_ring[0][0]()
    hop(first, 3)
    swapped(3)
    subs[3].begin()
    y_ring[1][1]()
    hop(first, 4)
    for g in first:
        g.arrived()
    cot_end()
    gy_phase(0, 0)
    y_ring[0][1]()
    hop(second, 1)
    gy_phase(0, 1)
    y_ring[1][2]()
    y_ring[0][2]()

    def mixed_copy(rel):
        o = lax.rem(y + rel, 4)
        slot = jnp.maximum(rel - 1, 0)
        return rcopy(mx_out.at[o], mx_in.at[slot], msend.at[slot], mrecv.at[slot], dev(z, k, o, x))

    def mixed_send(o):
        mixed_part(o)
        rel = lax.rem(o - y + 4, 4)

        @pl.when(rel != 0)
        def _():
            mixed_copy(rel).start()

    centre = (z + odd - x // 2 + 8) // 2

    def nth(n):
        return lax.rem(centre + jnp.where(odd == 1, (0, 3, 1, 2)[n], (0, 1, 3, 2)[n]), 4)

    hop(second, 2)
    for g in second:
        g.arrived(5)
    mixed_send(nth(0))
    hop(second, 3)
    for g in second:
        g.arrived(7)
    mixed_send(nth(1))
    hop(second, 4)
    for g in second:
        g.arrived()
    gy_phase(1, 0)
    mixed_send(nth(2))
    gy_tiles(1, 1)
    mixed_send(nth(3))

    def gy_sum(m):
        rows = TILES[m]
        for p in range(2):
            for rel in (1, 2, 3):
                gy_copy(p, lax.rem(x + rel, 4), m, rel).wait_recv()
            total = gy_out[p, x, rows, :].astype(F32)
            for r in range(3):
                total = total + gy_in[p, r, rows, :].astype(F32)
            gy_ref[rows, p * 256 : p * 256 + 256] = total.astype(BF)

    gy_sum(0)
    head = gy_ref[0:144, :].astype(F32)
    gz = head[0:136] * qs_ref[0:144, :].astype(F32)[0:136]
    gq = head[0:8] * z_ref[0:8, :]
    halo_ref[1, s_own] = jnp.concatenate(
        [gz, gq, ks_ref[0:16, :].astype(F32)[0:8], vs_ref[0:16, :].astype(F32)[0:8]], 0
    ).astype(BF)
    parts = halo_gathers(halo_ref.at[1], hsend.at[1], hrecv.at[1])
    for g in parts:
        g.begin()
    gy_send(1, 1)
    for n in (1, 2, 3):
        hop(parts, n)
    gy_sum(1)
    hop(parts, 4)

    for rel in (1, 2, 3):
        mixed_copy(jnp.int32(rel)).wait_recv()
        mixed_copy(jnp.int32(rel)).wait_send()

    @pl.loop(0, 4)
    def _(t):
        rows = pl.ds(pl.multiple_of(t * 128, 128), 128)
        total = mx_out[y, rows, :].astype(F32)
        for r in range(3):
            total = total + mx_in[r, rows, :].astype(F32)
        mixed_ref[rows, :] = total.astype(BF)

    for g in parts:
        g.arrived()
    next_ref[...] = halo_ref[1, holder(pack_ref, s_own, 1)]
    for g in parts:
        g.finish()
    for g in early + subs:
        g.finish()
    for copy in results:
        copy.wait()
    for c in sent:
        c.wait_send()


def products(*args):
    out = jax.ShapeDtypeStruct((TOK, CH), BF)
    dma = pltpu.SemaphoreType.DMA
    return pl.pallas_call(
        product_kernel,
        out_shape=[
            out,
            out,
            jax.ShapeDtypeStruct((MSG, CH), BF),
            jax.ShapeDtypeStruct((TOK, CH), F32),
            out,
            out,
            out,
            jax.ShapeDtypeStruct((256, CH), F32),
        ],
        in_specs=[sspec()] + [pl.BlockSpec(memory_space=pl.ANY)] * 3
        + [vspec()] * 6
        + [pl.BlockSpec(memory_space=pl.ANY)] * 3,
        out_specs=[vspec()] * 3 + [pl.BlockSpec(memory_space=pl.ANY)] * 5,
        scratch_shapes=[
            VM((4, 256, 256), BF),
            VM((4, 256, 256), BF),
            VM((4, 256, FILT), BF),
            VM((TOK, CH), F32),
            VM((TOK, CH), BF),
            VM((TOK, CH), BF),
            VM((TOK, CH), BF),
            VM((256, CH), F32),
            VM((3, TOK, CH), BF),
            VM((2, 16, MSG, CH), BF),
            VM((16, 512, 512), BF),
            VM((4, 512, 512), BF),
            VM((4, 512, 512), BF),
            VM((2, 4, 512, 256), BF),
            VM((2, 3, 512, 256), BF),
            VM((4, 512, 512), BF),
            VM((3, 512, 512), BF),
            VM((12, TOK + 8, 128), F32),
            VM((4, TOK + 8, 128), F32),
            VM((TOK, 128), F32),
            VM((TOK, 128), F32),
            dma((12,)),
            dma((2, SUBS)),
            dma((SUBS, 16)),
            dma((SUBS, 16)),
            dma((12,)),
            dma((12,)),
            dma((12,)),
            dma((12,)),
            dma((3,)),
            dma((3,)),
            dma((2, 3, 16)),
            dma((2, 3, 16)),
        ],
        compiler_params=pltpu.CompilerParams(
            collective_id=2, has_side_effects=True, vmem_limit_bytes=LIMIT
        ),
        name="products",
    )(*args)


def backward_kernel(
    back_ref, ahead_ref, halo_ref, gy_ref, z_ref, qs_ref, ks_ref, vs_ref, spec_ref, w_ref, row_ref,
    fwd_ref, inv_ref,
    grad_ref, gz_ext, g_ext, gu, reach,
):
    h = halo_ref[...].astype(F32)
    gz_ext[512:656, :] = h[0:144, :].astype(BF)
    gz_ext[656:768, :] = jnp.zeros((112, CH), BF)
    for g in range(4):
        g_ext[g, 512:520, :] = h[136:144, g * 128 : g * 128 + 128]

    @pl.loop(0, 8)
    def _(c):
        rows = pl.ds(pl.multiple_of(c * 64, 64), 64)
        gy = gy_ref[rows, :].astype(F32)
        gz_ext[rows, :] = (gy * qs_ref[rows, :].astype(F32)).astype(BF)
        gq = (gy * z_ref[rows, :]).astype(BF).astype(F32)
        for g in range(4):
            g_ext[g, rows, :] = gq[:, g * 128 : g * 128 + 128]

    rows_in = lax.broadcasted_iota(jnp.int32, (256, 256), 0)
    rows_out = lax.broadcasted_iota(jnp.int32, (128, 256), 0)

    def correlate(base, high, lanes, count):
        x = gz_ext[pl.ds(base, 256), lanes].astype(F32)
        x = jnp.where(rows_in < high, x, 0.0).astype(BF)
        spec = bdot(fwd_ref[...], x)
        xr, xi = spec[0:128], spec[128:256]
        hr, hi = spec_ref[0:128, lanes], spec_ref[128:256, lanes]
        prod = jnp.concatenate([xr * hr + xi * hi, xi * hr - xr * hi], 0).astype(BF)
        return bdot(inv_ref[0:count, :], prod)

    @pl.loop(0, 4)
    def _(b):
        base = pl.multiple_of(b * 128, 128)
        rows = pl.ds(base, 128)

        def one(t):
            stop = t + ahead_ref[t] + 1
            end = jnp.minimum(stop, base + 128)
            for half in range(2):
                lanes = pl.ds(half * 256, 256)
                out = correlate(base, stop - base, lanes, 128)
                keep = (rows_out >= t - base) & (rows_out < end - base)
                gu[:, lanes] = jnp.where(keep, out, gu[:, lanes])
            return end

        lax.while_loop(lambda t: t < base + 128, one, base)
        for g in range(4):
            lanes = pl.ds(g * 128, 128)
            part = gu[:, lanes]
            g_ext[4 + g, rows, :] = (part * vs_ref[rows, lanes].astype(F32)).astype(BF).astype(F32)
            g_ext[8 + g, rows, :] = (part * ks_ref[rows, lanes].astype(F32)).astype(BF).astype(F32)

    for half in range(2):
        lanes = pl.ds(half * 256, 256)
        part = correlate(512, ahead_ref[511], lanes, 16)
        gk = (part[0:8] * h[152:160, half * 256 : half * 256 + 256]).astype(BF).astype(F32)
        gv = (part[0:8] * h[144:152, half * 256 : half * 256 + 256]).astype(BF).astype(F32)
        for g in range(2):
            g_ext[4 + half * 2 + g, 512:520, :] = gk[:, g * 128 : g * 128 + 128]
            g_ext[8 + half * 2 + g, 512:520, :] = gv[:, g * 128 : g * 128 + 128]

    for c in range(8):
        start = c * 64

        def run(reach):
            for g in range(4):
                lanes = pl.ds(g * 128, 128)
                for s in range(3):
                    grad_ref[s, pl.ds(start, 64), lanes] = ahead_chunk(g_ext, s, start, w_ref, g, reach)

        both_ways(ahead_masked(back_ref, ahead_ref, start), row_ref, c // 2, c % 2, reach, run)


def backward(since, until, halo, gy, zed, qs, ks, vs, spec, short_filters, rows, fwd, inv):
    return pl.pallas_call(
        backward_kernel,
        in_specs=[sspec(), sspec()] + [vspec()] * 11,
        out_specs=vspec(),
        scratch_shapes=[
            VM((768, CH), BF),
            VM((12, TOK + 8, 128), F32),
            VM((128, CH), F32),
            VM((128, 128), F32),
        ],
        out_shape=jax.ShapeDtypeStruct((3, TOK, CH), BF),
        compiler_params=pltpu.CompilerParams(vmem_limit_bytes=LIMIT),
        name="backward_conv",
    )(since, until, halo, gy, zed, qs, ks, vs, spec, short_filters, rows, fwd, inv)


def body(proj, short_filters, long_filter, out_weight, cotangent, pack, since_start, until_end):
    fwd, inv_last, inv_first = dft_tables()
    back_rows = since_start.reshape(4, 128)
    ahead_rows = until_end.reshape(4, 128)
    mixed, gy, halo_next, zed, qs, ks, vs, spec = products(
        pack, out_weight, cotangent, proj, short_filters, long_filter, back_rows, ahead_rows,
        fwd, inv_last, *level_tables()
    )
    grad = backward(
        since_start, until_end, halo_next, gy, zed, qs, ks, vs, spec, short_filters, ahead_rows, fwd, inv_first
    )
    return (mixed, grad)


def solution(mesh):
    return jax.shard_map(
        body,
        mesh=mesh,
        in_specs=(
            P(None, "seq", "chan"),
            P(None, None, "chan"),
            P(None, "chan"),
            P("chan", "seq"),
            P("seq", "chan"),
            P(),
            P("seq"),
            P("seq"),
        ),
        out_specs=(P("seq", "chan"), P(None, "seq", "chan")),
        check_vma=False,
    )
```

```python
import functools

import jax
import jax.numpy as jnp
import numpy as np
from jax import lax
from jax.experimental import pallas as pl
from jax.experimental.pallas import tpu as pltpu
from jax.sharding import PartitionSpec as P

MESH = pl.DeviceIdType.MESH
BF = jnp.bfloat16
F32 = jnp.float32
TOK = 512
CH = 512
FILT = 128
SHORT = 7
MSG = 160
LIMIT = 56 << 20
VM = pltpu.VMEM


def vspec():
    return pl.BlockSpec(memory_space=pltpu.VMEM)


def sspec():
    return pl.BlockSpec(memory_space=pltpu.SMEM)


def dft_tables():
    k = np.arange(128)[:, None] + 0.5
    n = np.arange(256)[None, :]
    angle = 2 * np.pi * k * n / 256
    fwd = np.concatenate([np.cos(angle), -np.sin(angle)], 0)
    inv = np.concatenate([np.cos(angle), -np.sin(angle)], 0).T / 128
    return (
        jnp.asarray(fwd, BF),
        jnp.asarray(inv[128:], BF),
        jnp.asarray(inv[:128], BF),
    )


LEVELS = (64, 32, 16, 8)


def level_tables():
    fwd, inv, taps = [], [], []
    for run in LEVELS:
        pair = 2 * run
        k = np.arange(run)[:, None] + 0.5
        n = np.arange(pair)[None, :]
        angle = 2 * np.pi * k * n / pair
        cos, sin = np.cos(angle), np.sin(angle)
        first = (n < run).astype(np.float64)
        pairs = np.eye(256 // pair)
        fwd.append(np.concatenate([np.kron(pairs, cos * first), np.kron(pairs, -sin * first)], 0))
        last = 1.0 - first
        inv.append(
            np.concatenate([np.kron(pairs, cos * last), np.kron(pairs, -sin * last)], 0).T / run
        )
        wide = np.zeros((run, FILT))
        re, im = wide.copy(), wide.copy()
        re[:, :pair], im[:, :pair] = cos, -sin
        taps.append(np.concatenate([np.tile(re, (128 // run, 1)), np.tile(im, (128 // run, 1))], 0))
    return tuple(jnp.asarray(np.stack(t), BF) for t in (fwd, inv, taps))


def bdot(a, b):
    return jnp.dot(a, b, preferred_element_type=F32)


def reach_rows(row_ref, group):
    line = jnp.broadcast_to(row_ref[pl.ds(group, 1), :], (128, 128))
    return jnp.transpose(line.astype(F32))


def causal_chunk(ext, which, start, w_ref, g, reach):
    lanes = pl.ds(g * 128, 128)
    total = ext[which * 4 + g, pl.ds(start + 8, 64), :] * w_ref[which, 0:1, lanes]
    for i in range(1, SHORT):
        term = ext[which * 4 + g, pl.ds(start + 8 - i, 64), :] * w_ref[which, i : i + 1, lanes]
        if reach is not None:
            term = jnp.where(reach >= i, term, 0.0)
        total = total + term
    return total.astype(BF)


def ahead_chunk(ext, which, start, w_ref, g, reach):
    lanes = pl.ds(g * 128, 128)
    total = ext[which * 4 + g, pl.ds(start, 64), :] * w_ref[which, 0:1, lanes]
    for i in range(1, SHORT):
        term = ext[which * 4 + g, pl.ds(start + i, 64), :] * w_ref[which, i : i + 1, lanes]
        if reach is not None:
            term = jnp.where(reach >= i, term, 0.0)
        total = total + term
    return total.astype(BF)


def both_ways(is_masked, row_ref, group, half, reach, run):
    @pl.when(is_masked)
    def _():
        reach[...] = reach_rows(row_ref, group)
        run(reach[pl.ds(pl.multiple_of(half * 64, 64), 64), :])

    @pl.when(jnp.logical_not(is_masked))
    def _():
        run(None)


def ahead_masked(back_ref, ahead_ref, first):
    return (ahead_ref[first + 63] < SHORT - 1) | (back_ref[first + 63] < 63)


def place():
    s = lax.axis_index("seq")
    c = lax.axis_index("chan")
    return s // 2, s % 2, c // 4, c % 4


def dev(z, k, y, x):
    return (lax.rem(z + 8, 8) * 2 + k, lax.rem(y + 4, 4) * 4 + lax.rem(x + 4, 4))


def greet(targets):
    barrier = pltpu.get_barrier_semaphore()
    for t in targets:
        pl.semaphore_signal(barrier, inc=1, device_id=t, device_id_type=MESH)
    pl.semaphore_wait(barrier, len(targets))


def rcopy(src, dst, ssem, rsem, device):
    return pltpu.make_async_remote_copy(
        src_ref=src, dst_ref=dst, send_sem=ssem, recv_sem=rsem, device_id=device, device_id_type=MESH
    )


class SeqGather:
    def __init__(self, buf, r0, rows, send, recv):
        self.buf, self.r0, self.rows, self.send, self.recv = buf, r0, rows, send, recv
        self.z, self.k, self.y, self.x = place()
        self.sent = []
        self.from_sib = []
        self.seen = 0

    def view(self, z, k, part):
        s = lax.rem(z + 8, 8) * 2 + k
        half = self.rows // 2
        if part == 0:
            return self.buf.at[s, pl.ds(self.r0, self.rows)]
        return self.buf.at[s, pl.ds(self.r0 + (part - 1) * half, half)]

    def ring(self, way, hop):
        v = self.view(self.z - way * (hop - 1), self.k, 0 if hop < 4 else (1 if way > 0 else 2))
        n = (hop - 1) * 2 + (0 if way > 0 else 1)
        return rcopy(v, v, self.send.at[n], self.recv.at[n], dev(self.z + way, self.k, self.y, self.x))

    def landed(self, way, hop):
        v = self.view(self.z - way * hop, self.k, 0 if hop < 4 else (1 if way > 0 else 2))
        n = (hop - 1) * 2 + (0 if way > 0 else 1)
        rcopy(v, v, self.send.at[n], self.recv.at[n], dev(self.z + way, self.k, self.y, self.x)).wait_recv()

    def sib(self, offset, n):
        v = self.view(self.z + offset, self.k, 0)
        copy = rcopy(v, v, self.send.at[8 + n], self.recv.at[8 + n], dev(self.z, 1 - self.k, self.y, self.x))
        copy.start()
        self.sent.append(copy)
        w = self.view(self.z + offset, 1 - self.k, 0)
        self.from_sib.append(
            rcopy(w, w, self.send.at[8 + n], self.recv.at[8 + n], dev(self.z, 1 - self.k, self.y, self.x))
        )

    def go(self, way, hop):
        copy = self.ring(way, hop)
        copy.start()
        self.sent.append(copy)

    def begin(self):
        self.go(1, 1)
        self.go(-1, 1)
        self.sib(0, 0)

    def step(self, hop):
        for way in (1, -1):
            self.landed(way, hop)
            if hop < 4:
                self.go(way, hop + 1)
        if hop < 4:
            self.sib(-hop, 2 * hop - 1)
            self.sib(hop, 2 * hop)
        else:
            self.sib(4, 7)

    def arrived(self, count=8):
        while self.seen < count:
            self.from_sib[self.seen].wait_recv()
            self.seen += 1

    def finish(self):
        for copy in self.sent:
            copy.wait_send()


HALO_SUBS = ((0, 64), (64, 64), (128, 32))


def halo_gathers(buf, send, recv):
    return [SeqGather(buf, r0, rows, send.at[j], recv.at[j]) for j, (r0, rows) in enumerate(HALO_SUBS)]


def holder(pack_ref, seq, shift):
    wanted = pack_ref[seq] + shift
    found = jnp.int32(0)
    for i in range(16):
        found = found + jnp.where(pack_ref[i] == wanted, i, 0)
    return found


SUBS = 4
SUBROWS = 512 // SUBS
TILES = (pl.ds(0, 160), pl.ds(160, 352))


def product_kernel(
    pack_ref, w_ref, cot_own, proj_hbm, short_ref, long_ref, back_row, ahead_row,
    table_ref, inv_ref, lfwd_hbm, linv_hbm, ltaps_hbm,
    mixed_ref, gy_ref, next_ref, z_hbm, qs_hbm, ks_hbm, vs_hbm, spec_hbm,
    lfwd_ref, linv_ref, ltaps_ref, z_ref, qs_ref, ks_ref, vs_ref, spec_ref, proj_ref, halo_ref, w_all, cot_all, y_all, gy_out, gy_in, mx_out, mx_in, ext, u_ext, back_b, ahead_b,
    local, swap, wsend, wrecv, asend, arecv, gsend, grecv, msend, mrecv, hsend, hrecv,
):
    z, k, y, x = place()
    s_own = z * 2 + k
    column = lax.rem(s_own, 4)
    target = dev(z + jnp.where(x == 2, 1, 0) - jnp.where(x == 3, 1, 0), lax.rem(x, 2), y, column)
    odd = lax.rem(z + x // 2, 2)
    source = dev(z + odd * (2 * k - 1), lax.rem(x, 2), y, k + 2 * odd)
    stays = (lax.rem(z, 2) == 0) & (k == x)

    def slot(o, a):
        plane = 2 * o + x // 2 + jnp.where(a == 2, 1, 0) - jnp.where(a == 3, 1, 0)
        return lax.rem(plane + 8, 8) * 2 + lax.rem(a, 2)

    mine = [
        pltpu.make_async_copy(cot_own, cot_all.at[y], local.at[1]),
    ]
    streams = pltpu.make_async_copy(proj_hbm, proj_ref, local.at[3])
    for copy in mine:
        copy.start()
    streams.start()
    tables = [
        pltpu.make_async_copy(lfwd_hbm, lfwd_ref, local.at[4]),
        pltpu.make_async_copy(linv_hbm, linv_ref, local.at[5]),
        pltpu.make_async_copy(ltaps_hbm, ltaps_ref, local.at[6]),
    ]
    results = [
        pltpu.make_async_copy(z_ref, z_hbm, local.at[7]),
        pltpu.make_async_copy(qs_ref, qs_hbm, local.at[8]),
        pltpu.make_async_copy(ks_ref, ks_hbm, local.at[9]),
        pltpu.make_async_copy(vs_ref, vs_hbm, local.at[10]),
        pltpu.make_async_copy(spec_ref, spec_hbm, local.at[11]),
    ]
    for copy in tables:
        copy.start()
    barrier = pltpu.get_barrier_semaphore()
    for t in (
        dev(z + 1, k, y, x), dev(z - 1, k, y, x), dev(z, 1 - k, y, x),
        dev(z, k, y, x + 1), dev(z, k, y, x - 1), dev(z, k, y, x + 2),
        dev(z, k, y + 1, x), dev(z, k, y - 1, x), dev(z, k, y + 2, x),
    ):
        pl.semaphore_signal(barrier, inc=1, device_id=t, device_id_type=MESH)

    @pl.when(jnp.logical_not(stays))
    def _():
        for t in (target, source):
            pl.semaphore_signal(barrier, inc=1, device_id=t, device_id_type=MESH)


    sent = []

    def ring4(buf, me, at, base, r0, rows):
        def view(i, part):
            i = lax.rem(i + 4, 4)
            if part == 0:
                return buf.at[i, pl.ds(r0, rows)]
            return buf.at[i, pl.ds(r0 + (part - 1) * (rows // 2), rows // 2)]

        def copy(v, n, way):
            return rcopy(v, v, asend.at[base + n], arecv.at[base + n], at(way))

        def begin():
            for n, way in ((0, 1), (1, -1)):
                c = copy(view(me, 0), n, way)
                c.start()
                sent.append(c)

        def forward_on():
            for n, way in ((0, 1), (1, -1)):
                copy(view(me - way, 0), n, way).wait_recv()
                c = copy(view(me - way, 1 + n), 2 + n, way)
                c.start()
                sent.append(c)

        def end():
            for n, way in ((0, 1), (1, -1)):
                copy(view(me + 2, 1 + n), 2 + n, way).wait_recv()

        return begin, forward_on, end

    cot_begin, cot_on, cot_end = ring4(cot_all, y, lambda d: dev(z, k, y + d, x), 0, 0, 512)
    y_ring = [ring4(y_all, x, lambda d: dev(z, k, y, x + d), 4 + 4 * n, 256 * n, 256) for n in range(2)]

    subs = [SeqGather(w_all, j * SUBROWS, SUBROWS, wsend.at[j], wrecv.at[j]) for j in range(SUBS)]

    def gy_tile(p, a, m):
        rows = TILES[m]
        total = jnp.zeros((rows.size, 256), F32)
        for o in range(4):
            total = total + lax.dot_general(
                cot_all[o, rows, :], w_all[slot(o, a), pl.ds(p * 256, 256), :],
                (((1,), (1,)), ((), ())), preferred_element_type=F32,
            )
        gy_out[p, a, rows, :] = total.astype(BF)

    def gy_copy(p, a, m, rel):
        rows = TILES[m]
        n = (p * 2 + m) * 3 + rel - 1
        return rcopy(
            gy_out.at[p, a, rows], gy_in.at[p, rel - 1, rows], gsend.at[n], grecv.at[n], dev(z, k, y, a)
        )

    def mixed_part(o):
        @pl.loop(0, 4)
        def _(t):
            rows = pl.ds(pl.multiple_of((t // 2) * 256, 256), 256)
            cols = pl.ds(pl.multiple_of((t % 2) * 256, 256), 256)
            total = jnp.zeros((256, 256), F32)
            for a in range(4):
                total = total + bdot(y_all[a, rows, :], w_all[slot(o, a), :, cols])
            mx_out[o, rows, cols] = total.astype(BF)

    def gy_tiles(p, m):
        @pl.loop(0, 4)
        def _(i):
            rel = lax.rem(i + 1, 4)
            a = lax.rem(x + rel, 4)
            gy_tile(p, a, m)

    def gy_send(p, m):
        for rel in (2, 1, 3):
            c = gy_copy(p, lax.rem(x + rel, 4), m, rel)
            c.start()
            sent.append(c)

    def short_chunk(c):
        start = c * 64
        reach = back_b[start : start + 64, :]
        for g in range(4):
            lanes = pl.ds(g * 128, 128)
            got = [causal_chunk(ext, s, start, short_ref, g, reach) for s in range(3)]
            qs_ref[pl.ds(start, 64), lanes] = got[0]
            ks_ref[pl.ds(start, 64), lanes] = got[1]
            vs_ref[pl.ds(start, 64), lanes] = got[2]
            u_ext[g, pl.ds(start + 8, 64), :] = (got[1].astype(F32) * got[2].astype(F32)).astype(BF).astype(F32)

    def near_chunk(c):
        start = c * 64
        inside = lax.broadcasted_iota(jnp.int32, (64, 128), 0) % 8
        reach = jnp.minimum(back_b[start : start + 64, :], inside.astype(F32))
        for g in range(4):
            lanes = pl.ds(g * 128, 128)
            total = u_ext[g, pl.ds(start + 8, 64), :] * long_ref[0:1, lanes]
            for i in range(1, 8):
                term = u_ext[g, pl.ds(start + 8 - i, 64), :] * long_ref[i : i + 1, lanes]
                total = total + jnp.where(reach >= i, term, 0.0)
            z_ref[pl.ds(start, 64), lanes] = total

    def wide(mask):
        return jnp.concatenate([mask] * 2, axis=1)

    def times(spec, filt):
        n = spec.shape[0] // 2
        xr, xi, hr, hi = spec[:n], spec[n:], filt[:n], filt[n:]
        return jnp.concatenate([xr * hr - xi * hi, xr * hi + xi * hr], 0).astype(BF)

    def pairs_of_runs(batch):
        rows = pl.ds(batch * 256, 256)
        pos = lax.broadcasted_iota(jnp.int32, (256, 128), 0)

        @pl.loop(0, 4)
        def _(n):
            run = jnp.int32(64) >> n
            at = pos & (run - 1)
            second = (pos & run) != 0
            left = run - at
            into = jnp.where(
                jnp.logical_not(second) & (ahead_b[rows, :] >= left.astype(F32)), 1.0, 0.0
            )
            out = jnp.where(second & (back_b[rows, :] > at.astype(F32)), 1.0, 0.0)
            taps = bdot(ltaps_ref[n], long_ref[...].astype(BF))
            for half in range(2):
                lanes = pl.ds(half * 256, 256)
                u = jnp.concatenate(
                    [u_ext[half * 2 + g, pl.ds(batch * 256 + 8, 256), :] * into for g in range(2)], axis=1
                ).astype(BF)
                spec = bdot(lfwd_ref[n], u)
                prod = times(spec, taps[:, half * 256 : half * 256 + 256])
                z_ref[rows, lanes] += bdot(linv_ref[n], prod) * wide(out)

    def across(block, before):
        rows = pl.ds(block * 128, 128)
        pos = lax.broadcasted_iota(jnp.int32, (128, 128), 0)
        out = jnp.where(back_b[rows, :] > pos.astype(F32), 1.0, 0.0)
        for half in range(2):
            lanes = pl.ds(half * 256, 256)
            spec = bdot(table_ref[:, 0:128], before(half))
            prod = times(spec, spec_ref[:, lanes])
            z_ref[rows, lanes] += bdot(inv_ref[...], prod) * wide(out)

    def own_before(block):
        def get(half):
            pos = lax.broadcasted_iota(jnp.int32, (128, 128), 0)
            left = (128 - pos).astype(F32)
            into = jnp.where(ahead_b[pl.ds((block - 1) * 128, 128), :] >= left, 1.0, 0.0)
            return jnp.concatenate(
                [u_ext[half * 2 + g, pl.ds((block - 1) * 128 + 8, 128), :] * into for g in range(2)], axis=1
            ).astype(BF)

        return get

    def halo_before(half):
        pos = lax.broadcasted_iota(jnp.int32, (128, 128), 0)
        into = jnp.where(back_b[0:1, :] >= (128 - pos).astype(F32), 1.0, 0.0)
        return (got[0:128, half * 256 : half * 256 + 256].astype(F32) * wide(into)).astype(BF)

    def finish_y(batch):
        rows = pl.ds(batch * 256, 256)
        y_all[x, rows, :] = (qs_ref[rows, :].astype(F32) * z_ref[rows, :]).astype(BF)

    for g in range(4):
        back_b[g * 128 : g * 128 + 128, :] = reach_rows(back_row, g)
        ahead_b[g * 128 : g * 128 + 128, :] = reach_rows(ahead_row, g)
    streams.wait()
    for s in range(3):
        for g in range(4):
            ext[s * 4 + g, 8:520, :] = proj_ref[s, :, pl.ds(g * 128, 128)].astype(F32)
    for c in (7, 6):
        short_chunk(c)
    for g in range(4):
        lanes = pl.ds(g * 128, 128)
        halo_ref[0, s_own, 0:128, lanes] = u_ext[g, 392:520, :].astype(BF)
        halo_ref[0, s_own, 128:160, lanes] = jnp.concatenate(
            [ext[s * 4 + g, 512:520, :] for s in range(3)] + [jnp.zeros((8, 128), F32)], 0
        ).astype(BF)
    for copy in mine:
        copy.wait()

    @pl.when(jnp.logical_not(stays))
    def _():
        pl.semaphore_wait(barrier, 11)

    @pl.when(stays)
    def _():
        pl.semaphore_wait(barrier, 9)

    keep = pltpu.make_async_copy(w_ref, w_all.at[s_own], local.at[2])

    def swap_part(j, to):
        rows = pl.ds(j * SUBROWS, SUBROWS)
        return rcopy(w_ref.at[rows], w_all.at[to, rows], swap.at[0, j], swap.at[1, j], target)

    def swap_begin(parts):
        @pl.when(jnp.logical_not(stays))
        def _():
            for j in parts:
                swap_part(j, target[0]).start()

    @pl.when(stays)
    def _():
        keep.start()
        keep.wait()

    swap_begin((0, 1))
    early = halo_gathers(halo_ref.at[0], hsend.at[0], hrecv.at[0])
    for g in early:
        g.begin()
    def swapped(j):
        @pl.when(jnp.logical_not(stays))
        def _():
            swap_part(j, s_own).wait_recv()
            swap_part(j, target[0]).wait_send()

    def gy_phase(p, m):
        gy_tiles(p, m)
        gy_send(p, m)

    cot_begin()
    def hop(group, n):
        for g in group:
            g.step(n)

    first, second = subs[:2], subs[2:]
    for c in (5, 4):
        short_chunk(c)
    hop(early, 1)
    spec_ref[...] = bdot(table_ref[:, 0:128], long_ref[...].astype(BF))
    hop(early, 2)
    for j in range(2):
        swapped(j)
        subs[j].begin()
    swap_begin((2, 3))
    for c in (3, 2, 1):
        short_chunk(c)
    hop(early, 3)
    cot_on()
    for c in range(4, 8):
        near_chunk(c)
    for copy in tables:
        copy.wait()
    pairs_of_runs(1)
    hop(early, 4)
    hop(first, 1)
    across(2, own_before(2))
    across(3, own_before(3))
    finish_y(1)
    y_ring[1][0]()
    for g in early:
        g.arrived()
    got = halo_ref[0, holder(pack_ref, s_own, -1)]
    raw = got[128:160, :].astype(F32)
    for s in range(3):
        for g in range(4):
            ext[s * 4 + g, 0:8, :] = raw[s * 8 : s * 8 + 8, g * 128 : g * 128 + 128]
    short_chunk(0)
    hop(first, 2)
    swapped(2)
    subs[2].begin()
    for c in range(4):
        near_chunk(c)
    pairs_of_runs(0)
    across(0, halo_before)
    across(1, own_before(1))
    finish_y(0)
    for copy in results:
        copy.start()
    y_ring[0][0]()
    hop(first, 3)
    swapped(3)
    subs[3].begin()
    y_ring[1][1]()
    hop(first, 4)
    for g in first:
        g.arrived()
    cot_end()
    gy_phase(0, 0)
    y_ring[0][1]()
    hop(second, 1)
    gy_phase(0, 1)
    y_ring[1][2]()
    y_ring[0][2]()

    def mixed_copy(rel):
        o = lax.rem(y + rel, 4)
        slot = jnp.maximum(rel - 1, 0)
        return rcopy(mx_out.at[o], mx_in.at[slot], msend.at[slot], mrecv.at[slot], dev(z, k, o, x))

    def mixed_send(o):
        mixed_part(o)
        rel = lax.rem(o - y + 4, 4)

        @pl.when(rel != 0)
        def _():
            mixed_copy(rel).start()

    centre = (z + odd - x // 2 + 8) // 2

    def nth(n):
        return lax.rem(centre + jnp.where(odd == 1, (0, 3, 1, 2)[n], (0, 1, 3, 2)[n]), 4)

    hop(second, 2)
    for g in second:
        g.arrived(5)
    mixed_send(nth(0))
    hop(second, 3)
    for g in second:
        g.arrived(7)
    mixed_send(nth(1))
    hop(second, 4)
    for g in second:
        g.arrived()
    gy_phase(1, 0)
    mixed_send(nth(2))
    gy_tiles(1, 1)
    mixed_send(nth(3))

    def gy_sum(m):
        rows = TILES[m]
        for p in range(2):
            for rel in (1, 2, 3):
                gy_copy(p, lax.rem(x + rel, 4), m, rel).wait_recv()
            total = gy_out[p, x, rows, :].astype(F32)
            for r in range(3):
                total = total + gy_in[p, r, rows, :].astype(F32)
            gy_ref[rows, p * 256 : p * 256 + 256] = total.astype(BF)

    gy_sum(0)
    head = gy_ref[0:144, :].astype(F32)
    gz = head[0:136] * qs_ref[0:144, :].astype(F32)[0:136]
    gq = head[0:8] * z_ref[0:8, :]
    halo_ref[1, s_own] = jnp.concatenate(
        [gz, gq, ks_ref[0:16, :].astype(F32)[0:8], vs_ref[0:16, :].astype(F32)[0:8]], 0
    ).astype(BF)
    parts = halo_gathers(halo_ref.at[1], hsend.at[1], hrecv.at[1])
    for g in parts:
        g.begin()
    gy_send(1, 1)
    for n in (1, 2, 3):
        hop(parts, n)
    gy_sum(1)
    hop(parts, 4)

    for rel in (1, 2, 3):
        mixed_copy(jnp.int32(rel)).wait_recv()
        mixed_copy(jnp.int32(rel)).wait_send()

    @pl.loop(0, 4)
    def _(t):
        rows = pl.ds(pl.multiple_of(t * 128, 128), 128)
        total = mx_out[y, rows, :].astype(F32)
        for r in range(3):
            total = total + mx_in[r, rows, :].astype(F32)
        mixed_ref[rows, :] = total.astype(BF)

    for g in parts:
        g.arrived()
    next_ref[...] = halo_ref[1, holder(pack_ref, s_own, 1)]
    for g in parts:
        g.finish()
    for g in early + subs:
        g.finish()
    for copy in results:
        copy.wait()
    for c in sent:
        c.wait_send()


def products(*args):
    out = jax.ShapeDtypeStruct((TOK, CH), BF)
    dma = pltpu.SemaphoreType.DMA
    return pl.pallas_call(
        product_kernel,
        out_shape=[
            out,
            out,
            jax.ShapeDtypeStruct((MSG, CH), BF),
            jax.ShapeDtypeStruct((TOK, CH), F32),
            out,
            out,
            out,
            jax.ShapeDtypeStruct((256, CH), F32),
        ],
        in_specs=[sspec()] + [pl.BlockSpec(memory_space=pl.ANY)] * 3
        + [vspec()] * 6
        + [pl.BlockSpec(memory_space=pl.ANY)] * 3,
        out_specs=[vspec()] * 3 + [pl.BlockSpec(memory_space=pl.ANY)] * 5,
        scratch_shapes=[
            VM((4, 256, 256), BF),
            VM((4, 256, 256), BF),
            VM((4, 256, FILT), BF),
            VM((TOK, CH), F32),
            VM((TOK, CH), BF),
            VM((TOK, CH), BF),
            VM((TOK, CH), BF),
            VM((256, CH), F32),
            VM((3, TOK, CH), BF),
            VM((2, 16, MSG, CH), BF),
            VM((16, 512, 512), BF),
            VM((4, 512, 512), BF),
            VM((4, 512, 512), BF),
            VM((2, 4, 512, 256), BF),
            VM((2, 3, 512, 256), BF),
            VM((4, 512, 512), BF),
            VM((3, 512, 512), BF),
            VM((12, TOK + 8, 128), F32),
            VM((4, TOK + 8, 128), F32),
            VM((TOK, 128), F32),
            VM((TOK, 128), F32),
            dma((12,)),
            dma((2, SUBS)),
            dma((SUBS, 16)),
            dma((SUBS, 16)),
            dma((12,)),
            dma((12,)),
            dma((12,)),
            dma((12,)),
            dma((3,)),
            dma((3,)),
            dma((2, 3, 16)),
            dma((2, 3, 16)),
        ],
        compiler_params=pltpu.CompilerParams(
            collective_id=2, has_side_effects=True, vmem_limit_bytes=LIMIT
        ),
        name="products",
    )(*args)


def backward_kernel(
    back_ref, ahead_ref, halo_ref, gy_ref, z_ref, qs_ref, ks_hbm, vs_hbm, spec_hbm, w_ref, row_ref,
    fwd_ref, inv_ref,
    grad_hbm, gz_ext, g_ext, gu, reach, ks_ref, vs_ref, spec_ref, grad_ref, sem,
):
    loads = [
        pltpu.make_async_copy(ks_hbm, ks_ref, sem.at[0]),
        pltpu.make_async_copy(vs_hbm, vs_ref, sem.at[1]),
        pltpu.make_async_copy(spec_hbm, spec_ref, sem.at[2]),
    ]
    for copy in loads:
        copy.start()
    stores = [
        pltpu.make_async_copy(
            grad_ref.at[:, pl.ds(n * 256, 256), :], grad_hbm.at[:, pl.ds(n * 256, 256), :], sem.at[3 + n]
        )
        for n in range(2)
    ]
    h = halo_ref[...].astype(F32)
    gz_ext[512:656, :] = h[0:144, :].astype(BF)
    gz_ext[656:768, :] = jnp.zeros((112, CH), BF)
    for g in range(4):
        g_ext[g, 512:520, :] = h[136:144, g * 128 : g * 128 + 128]

    @pl.loop(0, 8)
    def _(c):
        rows = pl.ds(pl.multiple_of(c * 64, 64), 64)
        gy = gy_ref[rows, :].astype(F32)
        gz_ext[rows, :] = (gy * qs_ref[rows, :].astype(F32)).astype(BF)
        gq = (gy * z_ref[rows, :]).astype(BF).astype(F32)
        for g in range(4):
            g_ext[g, rows, :] = gq[:, g * 128 : g * 128 + 128]

    for copy in loads:
        copy.wait()
    rows_in = lax.broadcasted_iota(jnp.int32, (256, 256), 0)
    rows_out = lax.broadcasted_iota(jnp.int32, (128, 256), 0)

    def correlate(base, high, lanes, count):
        x = gz_ext[pl.ds(base, 256), lanes].astype(F32)
        x = jnp.where(rows_in < high, x, 0.0).astype(BF)
        spec = bdot(fwd_ref[...], x)
        xr, xi = spec[0:128], spec[128:256]
        hr, hi = spec_ref[0:128, lanes], spec_ref[128:256, lanes]
        prod = jnp.concatenate([xr * hr + xi * hi, xi * hr - xr * hi], 0).astype(BF)
        return bdot(inv_ref[0:count, :], prod)

    @pl.loop(0, 4)
    def _(b):
        base = pl.multiple_of(b * 128, 128)
        rows = pl.ds(base, 128)

        def one(t):
            stop = t + ahead_ref[t] + 1
            end = jnp.minimum(stop, base + 128)
            for half in range(2):
                lanes = pl.ds(half * 256, 256)
                out = correlate(base, stop - base, lanes, 128)
                keep = (rows_out >= t - base) & (rows_out < end - base)
                gu[:, lanes] = jnp.where(keep, out, gu[:, lanes])
            return end

        lax.while_loop(lambda t: t < base + 128, one, base)
        for g in range(4):
            lanes = pl.ds(g * 128, 128)
            part = gu[:, lanes]
            g_ext[4 + g, rows, :] = (part * vs_ref[rows, lanes].astype(F32)).astype(BF).astype(F32)
            g_ext[8 + g, rows, :] = (part * ks_ref[rows, lanes].astype(F32)).astype(BF).astype(F32)

    for half in range(2):
        lanes = pl.ds(half * 256, 256)
        part = correlate(512, ahead_ref[511], lanes, 16)
        gk = (part[0:8] * h[152:160, half * 256 : half * 256 + 256]).astype(BF).astype(F32)
        gv = (part[0:8] * h[144:152, half * 256 : half * 256 + 256]).astype(BF).astype(F32)
        for g in range(2):
            g_ext[4 + half * 2 + g, 512:520, :] = gk[:, g * 128 : g * 128 + 128]
            g_ext[8 + half * 2 + g, 512:520, :] = gv[:, g * 128 : g * 128 + 128]

    for c in range(8):
        start = c * 64

        def run(reach):
            for g in range(4):
                lanes = pl.ds(g * 128, 128)
                for s in range(3):
                    grad_ref[s, pl.ds(start, 64), lanes] = ahead_chunk(g_ext, s, start, w_ref, g, reach)

        both_ways(ahead_masked(back_ref, ahead_ref, start), row_ref, c // 2, c % 2, reach, run)
        if c % 4 == 3:
            stores[c // 4].start()
    for copy in stores:
        copy.wait()


def backward(since, until, halo, gy, zed, qs, ks, vs, spec, short_filters, rows, fwd, inv):
    return pl.pallas_call(
        backward_kernel,
        in_specs=[sspec(), sspec()] + [vspec()] * 4 + [pl.BlockSpec(memory_space=pl.ANY)] * 3 + [vspec()] * 4,
        out_specs=pl.BlockSpec(memory_space=pl.ANY),
        scratch_shapes=[
            VM((768, CH), BF),
            VM((12, TOK + 8, 128), F32),
            VM((128, CH), F32),
            VM((128, 128), F32),
            VM((TOK, CH), BF),
            VM((TOK, CH), BF),
            VM((256, CH), F32),
            VM((3, TOK, CH), BF),
            pltpu.SemaphoreType.DMA((5,)),
        ],
        out_shape=jax.ShapeDtypeStruct((3, TOK, CH), BF),
        compiler_params=pltpu.CompilerParams(vmem_limit_bytes=LIMIT),
        name="backward_conv",
    )(since, until, halo, gy, zed, qs, ks, vs, spec, short_filters, rows, fwd, inv)


def body(proj, short_filters, long_filter, out_weight, cotangent, pack, since_start, until_end):
    fwd, inv_last, inv_first = dft_tables()
    back_rows = since_start.reshape(4, 128)
    ahead_rows = until_end.reshape(4, 128)
    mixed, gy, halo_next, zed, qs, ks, vs, spec = products(
        pack, out_weight, cotangent, proj, short_filters, long_filter, back_rows, ahead_rows,
        fwd, inv_last, *level_tables()
    )
    grad = backward(
        since_start, until_end, halo_next, gy, zed, qs, ks, vs, spec, short_filters, ahead_rows, fwd, inv_first
    )
    return (mixed, grad)


def solution(mesh):
    return jax.shard_map(
        body,
        mesh=mesh,
        in_specs=(
            P(None, "seq", "chan"),
            P(None, None, "chan"),
            P(None, "chan"),
            P("chan", "seq"),
            P("seq", "chan"),
            P(),
            P("seq"),
            P("seq"),
        ),
        out_specs=(P("seq", "chan"), P(None, "seq", "chan")),
        check_vma=False,
    )
```
